128 devices in a mesh: feed: 16 (over y, z_hi, core), tm: 8 (over z_lo, x).
Axes of the slice: x: 4, y: 4, z: 4 (z_hi: 2, z_lo: 2; z = z_hi * 2 + z_lo), core: 2. Of those that a mesh axis runs over, the one named last changes fastest.
Arguments:
- samples: int32 [512, 524288], P('feed', 'tm'), may hold values from -8 to 7
- input_map: int32 [512], replicated, may hold values from 0 to 511, each once
Outputs:
- visibility: float32 [1024, 2, 512, 512], P(('feed', 'tm'))
The draws below stay inside these ranges and needn't reach their ends.
Inputs may be any that keep to these rules, and one draw needn't show every extreme that they name: `input_map`: each input appears once.
All inputs are finite; a program needn't handle non-finite values.
Results may differ from the reference program's by a relative error of at most 0.00055.
Values may be sent and summed in bfloat16 or wider, within the bound.
No kernel may reach another device: no remote copies, remote signals or barrier semaphores. Data moves between devices by JAX's collectives and lax.ppermute only.
A program may use at most 128 MiB of HBM per device.

```python
import math
import jax
import jax.numpy as jnp
from jax import lax

INPUTS = 512
CHANNELS = 1024
NFFT = 2048
TAPS = 4
FRAMES = 256
SAMPLES = 524288


def plant(drawn, rng, low, high):
    spot = [jax.random.randint(jax.random.fold_in(rng, axis), (), 0, length) for axis, length in enumerate(drawn.shape)]
    widest = drawn.shape.index(max(drawn.shape))
    next_to = spot[:widest] + [(spot[widest] + 1) % drawn.shape[widest]] + spot[widest + 1:]
    return drawn.at[tuple(spot)].set(low).at[tuple(next_to)].set(high)


def setup_inputs(seed: int = 0) -> dict:
    key_of = jax.random.split(jax.random.key(seed), 3)
    return {
        "samples": plant(jax.random.randint(key_of[0], (INPUTS, SAMPLES), -8, 8), jax.random.fold_in(key_of[0], 1), -8, 7).astype(jnp.int32),
        "input_map": jax.random.permutation(key_of[1], INPUTS).astype(jnp.int32),
    }


def taper_table():
    total = TAPS * NFFT
    place = jnp.arange(total).astype(jnp.float32)
    offset = (place - (total - 1) / 2.0) / NFFT
    values = jnp.sinc(offset) * (0.54 - 0.46 * jnp.cos(2.0 * math.pi * place / (total - 1)))
    return values.reshape(TAPS, NFFT).astype(jnp.float32)

def transform_table():
    sample = jnp.arange(NFFT).astype(jnp.int32)[:, None]
    channel = jnp.arange(CHANNELS).astype(jnp.int32)[None, :]
    phase = (sample * channel % NFFT).astype(jnp.float32) * (2.0 * math.pi / NFFT)
    factor = (8.0 * NFFT) ** (-0.5)
    pair = jnp.stack([jnp.cos(phase) * factor, -jnp.sin(phase) * factor], axis=-1)
    return pair.reshape(NFFT, 2 * CHANNELS).astype(jnp.bfloat16)

def reference(samples, input_map):
    wave = samples.astype(jnp.bfloat16).reshape(INPUTS, FRAMES, NFFT)
    before = jnp.zeros((INPUTS, TAPS - 1, NFFT), jnp.bfloat16)
    extended = jnp.concatenate([before, wave], axis=1)
    taper = taper_table()
    filtered = jnp.zeros((INPUTS, FRAMES, NFFT), jnp.float32)
    for tap in range(TAPS):
        filtered = filtered + taper[tap][None, None, :] * extended[:, tap:tap + FRAMES, :].astype(jnp.float32)
    filtered = filtered.astype(jnp.bfloat16)
    spectra = jnp.dot(filtered.reshape(INPUTS * FRAMES, NFFT), transform_table(), preferred_element_type=jnp.float32)
    spectra = spectra.astype(jnp.bfloat16).reshape(INPUTS, FRAMES, CHANNELS, 2)
    ordered = spectra[input_map]
    width = 8
    stacked = ordered.transpose(2, 3, 0, 1).reshape(CHANNELS // width, width, 2 * INPUTS, FRAMES)
    norm = 1.0 / math.sqrt(FRAMES)

    def correlate(block):
        wide = block.astype(jnp.float32)
        gram = jnp.einsum('cin,cjn->cij', wide, wide)
        real = (gram[:, :INPUTS, :INPUTS] + gram[:, INPUTS:, INPUTS:]) * norm
        imag = (gram[:, INPUTS:, :INPUTS] - gram[:, :INPUTS, INPUTS:]) * norm
        return jnp.stack([real, imag], axis=1)
    result = lax.map(correlate, stacked)
    return result.reshape(CHANNELS, 2, INPUTS, INPUTS)
```

```python
import functools
import math

import jax
import jax.numpy as jnp
import ml_dtypes
import numpy as np
from jax import lax
from jax.experimental import pallas as pl
from jax.experimental.pallas import tpu as pltpu
from jax.sharding import PartitionSpec as P

CHANNELS = 1024
NFFT = 2048
TAPS = 4
HALO = TAPS - 1
LANES = 128
GROUP = 8
TILE = 256
CHUNKS = (8,)
VMEM = 56 * 1024 * 1024


def taper_table():
    total = TAPS * NFFT
    place = np.arange(total).astype(np.float32)
    offset = (place - np.float32((total - 1) / 2.0)) / np.float32(NFFT)
    arg = np.float32(math.pi) * offset
    sinc = np.sin(arg) / arg
    window = np.float32(0.54) - np.float32(0.46) * np.cos(
        np.float32(2.0 * math.pi) * place / np.float32(total - 1)
    )
    return (sinc * window).astype(np.float32).reshape(TAPS, NFFT)


def transform_table(devices, first, count):
    per = CHANNELS // devices
    sample = np.arange(NFFT)[None, :]
    channel = (np.arange(devices)[:, None] * per + first + np.arange(count)[None, :]).reshape(-1, 1)
    phase = (sample * channel % NFFT).astype(np.float32) * np.float32(2.0 * math.pi / NFFT)
    factor = np.float32((8.0 * NFFT) ** (-0.5))
    pair = np.stack([np.cos(phase) * factor, -np.sin(phase) * factor], axis=1)
    return pair.reshape(2 * devices * count, NFFT).astype(ml_dtypes.bfloat16)


def filter_kernel(frames, samples_ref, halo_ref, taper_ref, out_ref, carry_ref):
    step = pl.program_id(0)

    @pl.when(step == 0)
    def _():
        carry_ref[...] = halo_ref[...].astype(jnp.float32)

    rows = samples_ref.shape[0]

    def columns(chunk, _):
        start = pl.multiple_of(chunk * LANES, LANES)
        taper = [taper_ref[tap, pl.ds(start, LANES)][None, :] for tap in range(TAPS)]
        for row in range(0, rows, 16):
            part = pl.ds(row, 16)
            x = [carry_ref[part, pl.ds(start + t * NFFT, LANES)] for t in range(HALO)]
            for k in range(frames):
                x.append(samples_ref[part, pl.ds(start + k * NFFT, LANES)].astype(jnp.float32))
                value = taper[0] * x[k]
                for tap in range(1, TAPS):
                    value = value + taper[tap] * x[k + tap]
                out_ref[pl.ds(k * rows + row, 16), pl.ds(start, LANES)] = value.astype(jnp.bfloat16)
            for t in range(HALO):
                carry_ref[part, pl.ds(start + t * NFFT, LANES)] = x[frames + t]
        return 0

    lax.fori_loop(0, NFFT // LANES, columns, 0)


def filtered_frames(samples, halo, taper):
    rows, length = samples.shape
    steps = length // (GROUP * NFFT)
    return pl.pallas_call(
        functools.partial(filter_kernel, GROUP),
        grid=(steps,),
        in_specs=[
            pl.BlockSpec((rows, GROUP * NFFT), lambda i: (0, i)),
            pl.BlockSpec((rows, HALO * NFFT), lambda i: (0, 0)),
            pl.BlockSpec((TAPS, NFFT), lambda i: (0, 0)),
        ],
        out_specs=pl.BlockSpec((GROUP * rows, NFFT), lambda i: (i, 0)),
        out_shape=jax.ShapeDtypeStruct((rows * length // NFFT, NFFT), jnp.bfloat16),
        scratch_shapes=[pltpu.VMEM((rows, HALO * NFFT), jnp.float32)],
        compiler_params=pltpu.CompilerParams(vmem_limit_bytes=VMEM),
        cost_estimate=pl.CostEstimate(
            flops=8 * rows * length, bytes_accessed=6 * rows * length, transcendentals=0
        ),
        name="filter",
    )(samples, halo, taper)


def transform_kernel(table_ref, filtered_ref, out_ref, turn_ref):
    value = lax.dot_general(
        table_ref[...],
        filtered_ref[...],
        (((1,), (1,)), ((), ())),
        preferred_element_type=jnp.float32,
    )
    count = value.shape[1] // LANES
    for j in range(count):
        turn_ref[pl.ds(j, value.shape[0], stride=count), :] = value[:, j * LANES : (j + 1) * LANES]
    out_ref[...] = turn_ref[...].astype(jnp.bfloat16).reshape(out_ref.shape)


def transformed(table, filtered, devices, count):
    total = filtered.shape[0]
    per = total // LANES
    rows = 2 * devices * count
    return pl.pallas_call(
        transform_kernel,
        grid=(rows // TILE,),
        in_specs=[
            pl.BlockSpec((TILE, NFFT), lambda i: (i, 0)),
            pl.BlockSpec((total, NFFT), lambda i: (0, 0)),
        ],
        out_specs=pl.BlockSpec(
            (TILE // (2 * count), count, 2 * per, LANES), lambda i: (i, 0, 0, 0)
        ),
        out_shape=jax.ShapeDtypeStruct((devices, count, 2 * per, LANES), jnp.bfloat16),
        scratch_shapes=[pltpu.VMEM((TILE * per, LANES), jnp.float32)],
        compiler_params=pltpu.CompilerParams(vmem_limit_bytes=VMEM),
        cost_estimate=pl.CostEstimate(
            flops=2 * rows * NFFT * total,
            bytes_accessed=2 * (rows * NFFT + total * NFFT + rows * total),
            transcendentals=0,
        ),
        name="transform",
    )(table, filtered)


def gram_kernel(feeds, times, norm, x_ref, place_ref, *refs):
    out_ref, turned_ref, z_ref = refs[-3:]
    per = x_ref.shape[2] // 2
    inputs = place_ref.shape[0]
    block = inputs // feeds
    inner = LANES // block
    high = times * per
    frames = inner * high
    for first in range(0, feeds, inner):
        parts = []
        for f in range(first, first + inner):
            x = x_ref[f * times : (f + 1) * times, 0].astype(jnp.float32)
            x = x.reshape(times, 2, per, LANES)
            parts.append([x[:, r].reshape(high, LANES) for r in range(2)])
        for r in range(2):
            for k in range(inner):
                side = jnp.concatenate(
                    [part[r][:, k * block : (k + 1) * block] for part in parts], axis=1
                )
                turned_ref[
                    r * frames + k * high : r * frames + (k + 1) * high,
                    first * block : (first + inner) * block,
                ] = side.astype(jnp.bfloat16)
    z = lax.dot_general(
        place_ref[...],
        turned_ref[...],
        (((1,), (1,)), ((), ())),
        preferred_element_type=jnp.float32,
    )
    z_ref[0] = z.astype(jnp.bfloat16)
    z_ref[1, :, :frames] = z[:, frames:].astype(jnp.bfloat16)
    z_ref[1, :, frames:] = (-z[:, :frames]).astype(jnp.bfloat16)
    for r in range(2):
        out_ref[0, r] = norm * lax.dot_general(
            z_ref[r], z_ref[0], (((1,), (1,)), ((), ())), preferred_element_type=jnp.float32
        )


def grams(incoming, place, previous, first, channels, feeds, times):
    count, per = incoming.shape[1], incoming.shape[2] // 2
    inputs = place.shape[0]
    frames = times * per * LANES * feeds // inputs
    in_specs = [
        pl.BlockSpec((feeds * times, 1, 2 * per, LANES), lambda c: (0, c, 0, 0)),
        pl.BlockSpec((inputs, inputs), lambda c: (0, 0)),
    ]
    args = [incoming, place]
    aliases = {}
    if previous is not None:
        in_specs.append(pl.BlockSpec(memory_space=pl.ANY))
        args.append(previous)
        aliases = {2: 0}
    return pl.pallas_call(
        functools.partial(gram_kernel, feeds, times, 1.0 / math.sqrt(frames)),
        grid=(count,),
        in_specs=in_specs,
        out_specs=pl.BlockSpec((1, 2, inputs, inputs), lambda c: (first + c, 0, 0, 0)),
        out_shape=jax.ShapeDtypeStruct((channels, 2, inputs, inputs), jnp.float32),
        scratch_shapes=[
            pltpu.VMEM((2 * frames, inputs), jnp.bfloat16),
            pltpu.VMEM((2, inputs, 2 * frames), jnp.bfloat16),
        ],
        input_output_aliases=aliases,
        compiler_params=pltpu.CompilerParams(vmem_limit_bytes=VMEM),
        cost_estimate=pl.CostEstimate(
            flops=count * 12 * inputs * inputs * frames,
            bytes_accessed=count * (8 * inputs * inputs + 4 * inputs * frames),
            transcendentals=0,
        ),
        name="gram",
    )(*args)


def per_device(samples, input_map):
    feeds = lax.axis_size("feed")
    times = lax.axis_size("tm")
    devices = feeds * times
    channels = CHANNELS // devices
    tail = samples[:, samples.shape[1] - HALO * NFFT :].astype(jnp.bfloat16)
    halo = lax.ppermute(tail, "tm", [(t, t + 1) for t in range(times - 1)])
    filtered = filtered_frames(samples, halo, jnp.asarray(taper_table()))
    inputs = input_map.shape[0]
    place = (input_map[:, None] == jnp.arange(inputs)[None, :]).astype(jnp.bfloat16)
    result = None
    first = 0
    arrived = []
    for count in CHUNKS:
        table = jnp.asarray(transform_table(devices, first, count))
        outgoing = transformed(table, filtered, devices, count)
        incoming = lax.all_to_all(
            outgoing, ("feed", "tm"), split_axis=0, concat_axis=0, tiled=True
        )
        arrived.append((first, incoming))
        first += count
    for first, incoming in arrived:
        result = grams(incoming, place, result, first, channels, feeds, times)
    return result


def solution(mesh):
    in_specs = (P("feed", "tm"), P())
    out_specs = P(("feed", "tm"), None, None, None)
    return jax.shard_map(
        per_device, mesh=mesh, in_specs=in_specs, out_specs=out_specs, check_vma=False
    )
```

```python
import functools
import math

import jax
import jax.numpy as jnp
import ml_dtypes
import numpy as np
from jax import lax
from jax.experimental import pallas as pl
from jax.experimental.pallas import tpu as pltpu
from jax.sharding import PartitionSpec as P

CHANNELS = 1024
NFFT = 2048
TAPS = 4
HALO = TAPS - 1
LANES = 128
GROUP = 8
PAIR = 2
TILE = 1024
MIB = 1024 * 1024


def taper_table():
    total = TAPS * NFFT
    place = np.arange(total).astype(np.float32)
    offset = (place - np.float32((total - 1) / 2.0)) / np.float32(NFFT)
    arg = np.float32(math.pi) * offset
    sinc = np.sin(arg) / arg
    window = np.float32(0.54) - np.float32(0.46) * np.cos(
        np.float32(2.0 * math.pi) * place / np.float32(total - 1)
    )
    return (sinc * window).astype(np.float32).reshape(TAPS, NFFT)


def transform_table():
    sample = np.arange(NFFT)[None, :]
    channel = np.arange(CHANNELS)[:, None]
    phase = (sample * channel % NFFT).astype(np.float32) * np.float32(2.0 * math.pi / NFFT)
    factor = np.float32((8.0 * NFFT) ** (-0.5))
    pair = np.stack([np.cos(phase) * factor, -np.sin(phase) * factor], axis=1)
    return pair.reshape(2 * CHANNELS, NFFT).astype(ml_dtypes.bfloat16)


def filter_columns(samples_ref, past, taper_ref, out_ref, chunk, frames, carry_ref=None):
    rows = samples_ref.shape[0]
    start = pl.multiple_of(chunk * LANES, LANES)
    taper = [taper_ref[pl.ds(tap, 1), pl.ds(start, LANES)] for tap in range(TAPS)]
    for row in range(0, rows, 16):
        part = pl.ds(row, 16)
        x = [past(t, part, start) for t in range(HALO)]
        for k in range(frames):
            x.append(samples_ref[part, pl.ds(start + k * NFFT, LANES)].astype(jnp.float32))
            value = taper[0] * x[k]
            for tap in range(1, TAPS):
                value = value + taper[tap] * x[k + tap]
            out_ref[pl.ds(k * rows + row, 16), pl.ds(start, LANES)] = value.astype(jnp.bfloat16)
        if carry_ref is not None:
            for t in range(HALO):
                carry_ref[part, pl.ds(start + t * NFFT, LANES)] = x[frames + t]


def transform_tile(table, filtered, turn_ref):
    value = lax.dot_general(
        table, filtered, (((1,), (1,)), ((), ())), preferred_element_type=jnp.float32
    )
    count = value.shape[1] // LANES
    for j in range(count):
        turn_ref[pl.ds(j, value.shape[0], stride=count), :] = value[:, j * LANES : (j + 1) * LANES]
    return turn_ref[...].astype(jnp.bfloat16)


def head_kernel(
    samples_ref, before_ref, taper_ref, table_ref, out_ref, first_ref,
    held_ref, carry_ref, even_ref, odd_ref, turn_ref, sems,
):
    step = pl.program_id(0)
    tiles = table_ref.shape[0] // TILE
    share = NFFT // LANES // tiles
    devices = out_ref.shape[0] // tiles

    def fetch(m):
        part = pl.ds(m * TILE, TILE)
        return pltpu.make_async_copy(table_ref.at[part], held_ref.at[part], sems.at[m])

    def past(t, part, start):
        return carry_ref[part, pl.ds(start + t * NFFT, LANES)]

    def past_first(t, part, start):
        lanes = pl.ds(start + (t + 1) * NFFT, LANES)
        return before_ref[part, lanes].astype(jnp.float32)

    @pl.when(step == 0)
    def _():
        for m in range(tiles):
            fetch(m).start()

        def body(m, _):
            for n in range(share):
                filter_columns(
                    samples_ref, past_first, taper_ref, even_ref, m * share + n, GROUP, carry_ref
                )
            return 0

        lax.fori_loop(0, tiles, body, 0)

    def both(now_ref, next_ref, wait):
        def body(m, _):
            if wait:
                fetch(m).wait()
            row = pl.multiple_of(m * TILE, TILE)
            tile = transform_tile(held_ref[pl.ds(row, TILE), :], now_ref[...], turn_ref)
            out_ref[pl.ds(m * devices, devices)] = tile.reshape((devices,) + out_ref.shape[1:])
            for n in range(share):
                filter_columns(
                    samples_ref, past, taper_ref, next_ref, m * share + n, GROUP, carry_ref
                )
            return 0

        lax.fori_loop(0, tiles, body, 0)

    pl.when(step == 1)(lambda: both(even_ref, odd_ref, True))
    pl.when(step == 2)(lambda: both(odd_ref, even_ref, False))
    pl.when(step == 3)(lambda: both(even_ref, first_ref, False))


def head(samples, taper, table, devices):
    rows, length = samples.shape
    groups = length // (GROUP * NFFT)
    assert groups == 4
    pairs = CHANNELS // devices // PAIR
    sub = PAIR * 2 * GROUP * rows // (LANES * PAIR * 2) * PAIR * 2
    spectra = (devices, pairs, groups, sub, LANES)
    width = GROUP * rows
    return pl.pallas_call(
        head_kernel,
        grid=(groups,),
        in_specs=[
            pl.BlockSpec((rows, GROUP * NFFT), lambda s: (0, (s + 1) % groups)),
            pl.BlockSpec((rows, 4 * NFFT), lambda s: (0, 1)),
            pl.BlockSpec((TAPS, NFFT), lambda s: (0, 0)),
            pl.BlockSpec(memory_space=pl.ANY),
        ],
        out_specs=[
            pl.BlockSpec(
                (devices, pairs, None, sub, LANES), lambda s: (0, 0, jnp.maximum(s, 1), 0, 0)
            ),
            pl.BlockSpec((width, NFFT), lambda s: (0, 0)),
        ],
        out_shape=[
            jax.ShapeDtypeStruct(spectra, jnp.bfloat16),
            jax.ShapeDtypeStruct((width, NFFT), jnp.bfloat16),
        ],
        scratch_shapes=[
            pltpu.VMEM(table.shape, jnp.bfloat16),
            pltpu.VMEM((rows, HALO * NFFT), jnp.float32),
            pltpu.VMEM((width, NFFT), jnp.bfloat16),
            pltpu.VMEM((width, NFFT), jnp.bfloat16),
            pltpu.VMEM((TILE * width // LANES, LANES), jnp.float32),
            pltpu.SemaphoreType.DMA((table.shape[0] // TILE,)),
        ],
        compiler_params=pltpu.CompilerParams(vmem_limit_bytes=60 * MIB),
        cost_estimate=pl.CostEstimate(
            flops=2 * table.shape[0] * NFFT * width * 3,
            bytes_accessed=2 * table.shape[0] * NFFT + 4 * rows * length,
            transcendentals=0,
        ),
        name="head",
    )(samples, samples, taper, table)


def tail_kernel(
    samples_ref, halo_ref, first_ref, taper_ref, table_ref, _, out_ref, filtered_ref, turn_ref
):
    rows = samples_ref.shape[0]

    @pl.when(pl.program_id(0) == 0)
    def _():
        keep = HALO * rows
        filtered_ref[keep:, :] = first_ref[keep:, :]

        def past(t, part, start):
            return halo_ref[part, pl.ds(start + t * NFFT, LANES)].astype(jnp.float32)

        def body(chunk, _):
            filter_columns(samples_ref, past, taper_ref, filtered_ref, chunk, HALO)
            return 0

        lax.fori_loop(0, NFFT // LANES, body, 0)

    tile = transform_tile(table_ref[...], filtered_ref[...], turn_ref)
    out_ref[...] = tile.reshape(out_ref.shape)


def tail(samples, halo, first, taper, table, spectra):
    rows = samples.shape[0]
    width = GROUP * rows
    devices, pairs, groups, sub, _ = spectra.shape
    tiles = table.shape[0] // TILE
    return pl.pallas_call(
        tail_kernel,
        grid=(tiles,),
        in_specs=[
            pl.BlockSpec((rows, HALO * NFFT), lambda m: (0, 0)),
            pl.BlockSpec((rows, HALO * NFFT), lambda m: (0, 0)),
            pl.BlockSpec((width, NFFT), lambda m: (0, 0)),
            pl.BlockSpec((TAPS, NFFT), lambda m: (0, 0)),
            pl.BlockSpec((TILE, NFFT), lambda m: (m, 0)),
            pl.BlockSpec(memory_space=pl.ANY),
        ],
        out_specs=pl.BlockSpec(
            (devices // tiles, pairs, None, sub, LANES), lambda m: (m, 0, 0, 0, 0)
        ),
        out_shape=jax.ShapeDtypeStruct(spectra.shape, spectra.dtype),
        scratch_shapes=[
            pltpu.VMEM((width, NFFT), jnp.bfloat16),
            pltpu.VMEM((TILE * width // LANES, LANES), jnp.float32),
        ],
        input_output_aliases={5: 0},
        compiler_params=pltpu.CompilerParams(vmem_limit_bytes=60 * MIB),
        cost_estimate=pl.CostEstimate(
            flops=2 * table.shape[0] * NFFT * width,
            bytes_accessed=2 * table.shape[0] * NFFT,
            transcendentals=0,
        ),
        name="tail",
    )(samples, halo, first, taper, table, spectra)


def lane_turn(parts, block):
    lane = lax.broadcasted_iota(jnp.int32, parts[0].shape, 1)
    for step in (2, 1):
        upper = (lane // (block * step)) % 2 == 1
        turned = list(parts)
        for p in range(4):
            if p & step:
                continue
            low, high = parts[p], parts[p + step]
            turned[p] = jnp.where(upper, pltpu.roll(high, step * block, 1), low)
            turned[p + step] = jnp.where(upper, high, pltpu.roll(low, LANES - step * block, 1))
        parts = turned
    return parts


def spread(x, wide_ref):
    wide_ref[...] = x.astype(jnp.float32).reshape(wide_ref.shape)


def arrange(wide_ref, turned_ref, channel, feeds):
    each = wide_ref.shape[0] // feeds
    high = each // 8
    block = turned_ref.shape[1] // feeds
    inner = LANES // block
    half = turned_ref.shape[0] // 2
    for first in range(0, feeds, inner):
        for r in range(2):
            parts = []
            for f in range(first, first + inner):
                start = f * each + 4 * channel + 2 * r
                both = [wide_ref[pl.ds(start + j, high, stride=8), :] for j in range(2)]
                parts.append(jnp.concatenate(both, axis=0).astype(jnp.bfloat16))
            for k, side in enumerate(lane_turn(parts, block)):
                row = r * half + 2 * k * high
                turned_ref[row : row + 2 * high, first * block : (first + inner) * block] = side


def product(a, b):
    return lax.dot_general(a, b, (((1,), (1,)), ((), ())), preferred_element_type=jnp.float32)


def order(turned_ref, place_ref, z_ref):
    inputs = place_ref.shape[0]
    frames = turned_ref.shape[0] // 2
    z = product(place_ref[...], turned_ref[...])
    z_ref[:inputs] = z.astype(jnp.bfloat16)
    z_ref[inputs:, :frames] = z[:, frames:].astype(jnp.bfloat16)
    z_ref[inputs:, frames:] = (-z[:, :frames]).astype(jnp.bfloat16)


def correlate(z_ref, out_ref, norm):
    inputs = z_ref.shape[1]
    value = norm * product(z_ref[...], z_ref[:inputs])
    out_ref[0] = value[:inputs]
    out_ref[1] = value[inputs:]


def gram_kernel(
    feeds, norm, x_ref, place_ref, out_ref, held_ref, wide_ref, turned0_ref, turned1_ref,
    z0_ref, z1_ref, done0_ref, done1_ref, in_sems, out_sems,
):
    turned, z, done = (turned0_ref, turned1_ref), (z0_ref, z1_ref), (done0_ref, done1_ref)
    pairs = x_ref.shape[1]

    def fetch(pair):
        return pltpu.make_async_copy(x_ref.at[:, pair], held_ref.at[pair], in_sems.at[pair])

    def send(channel, parity):
        return pltpu.make_async_copy(done[parity], out_ref.at[channel], out_sems.at[parity])

    def phase(pair, parity, third=True, second=True, first=True, wait=True):
        channel = PAIR * pair + parity
        if first and parity == 0:
            fetch(pair).wait()
        if third:
            if wait:
                send(channel - 4, parity).wait()
            correlate(z[parity], done[parity], norm)
        if second:
            order(turned[1 - parity], place_ref, z[1 - parity])
        if first:
            if parity == 0:
                spread(held_ref[pair], wide_ref)
            arrange(wide_ref, turned[parity], parity, feeds)
        if third:
            send(channel - 2, parity).start()

    for pair in range(pairs):
        fetch(pair).start()
    phase(0, 0, third=False, second=False)
    phase(0, 1, third=False)
    phase(1, 0, wait=False)
    phase(1, 1, wait=False)

    def body(pair, _):
        phase(pair, 0)
        phase(pair, 1)
        return 0

    lax.fori_loop(2, pairs, body, 0)
    phase(pairs, 0, first=False)
    phase(pairs, 1, second=False, first=False)
    for parity in range(PAIR):
        send(PAIR * pairs - 2 + parity, parity).wait()


def grams(incoming, place, feeds):
    devices, pairs, groups, sub, _ = incoming.shape
    channels = PAIR * pairs
    inputs = place.shape[0]
    frames = devices * groups * sub * LANES // (2 * PAIR * inputs)
    return pl.pallas_call(
        functools.partial(gram_kernel, feeds, 1.0 / math.sqrt(frames)),
        in_specs=[
            pl.BlockSpec(memory_space=pl.ANY),
            pl.BlockSpec(memory_space=pltpu.VMEM),
        ],
        out_specs=pl.BlockSpec(memory_space=pl.ANY),
        out_shape=jax.ShapeDtypeStruct((channels, 2, inputs, inputs), jnp.float32),
        scratch_shapes=[
            pltpu.VMEM((pairs, devices, groups, sub, LANES), jnp.bfloat16),
            pltpu.VMEM((devices * groups * sub, LANES), jnp.float32),
            pltpu.VMEM((2 * frames, inputs), jnp.bfloat16),
            pltpu.VMEM((2 * frames, inputs), jnp.bfloat16),
            pltpu.VMEM((2 * inputs, 2 * frames), jnp.bfloat16),
            pltpu.VMEM((2 * inputs, 2 * frames), jnp.bfloat16),
            pltpu.VMEM((2, inputs, inputs), jnp.float32),
            pltpu.VMEM((2, inputs, inputs), jnp.float32),
            pltpu.SemaphoreType.DMA((pairs,)),
            pltpu.SemaphoreType.DMA((PAIR,)),
        ],
        compiler_params=pltpu.CompilerParams(vmem_limit_bytes=60 * MIB),
        cost_estimate=pl.CostEstimate(
            flops=channels * 12 * inputs * inputs * frames,
            bytes_accessed=channels * (8 * inputs * inputs + 4 * inputs * frames),
            transcendentals=0,
        ),
        name="gram",
    )(incoming, place)


def per_device(samples, input_map):
    feeds = lax.axis_size("feed")
    times = lax.axis_size("tm")
    devices = feeds * times
    inputs = input_map.shape[0]
    taper = jnp.asarray(taper_table())
    table = jnp.asarray(transform_table())
    last = samples[:, samples.shape[1] - HALO * NFFT :].astype(jnp.bfloat16)
    halo = lax.ppermute(last, "tm", [(t, t + 1) for t in range(times - 1)])
    place = (input_map[:, None] == jnp.arange(inputs)[None, :]).astype(jnp.bfloat16)
    spectra, first = head(samples, taper, table, devices)
    outgoing = tail(samples, halo, first, taper, table, spectra)
    incoming = lax.all_to_all(outgoing, ("feed", "tm"), split_axis=0, concat_axis=0, tiled=True)
    return grams(incoming, place, feeds)


def solution(mesh):
    in_specs = (P("feed", "tm"), P())
    out_specs = P(("feed", "tm"), None, None, None)
    return jax.shard_map(
        per_device, mesh=mesh, in_specs=in_specs, out_specs=out_specs, check_vma=False
    )
```

```python
import functools
import math

import jax
import jax.numpy as jnp
import ml_dtypes
import numpy as np
from jax import lax
from jax.experimental import pallas as pl
from jax.experimental.pallas import tpu as pltpu
from jax.sharding import PartitionSpec as P

CHANNELS = 1024
NFFT = 2048
HALF = NFFT // 2
TAPS = 4
HALO = TAPS - 1
LANES = 128
GROUP = 8
PAIR = 2
SLOTS = (0, 4, 1, 7, 2, 6, 3, 5)
EXTRA = 16
PARTS = (528, 512)
MIB = 1024 * 1024


def sample_order():
    chunk = 2 * LANES * np.arange(HALF // LANES)[:, None]
    lane = np.arange(LANES)[None, :]
    even = chunk + 2 * lane
    odd = chunk + (LANES + 2 * lane) % (2 * LANES) + 1
    return np.concatenate([even.reshape(-1), odd.reshape(-1)])


def taper_table():
    total = TAPS * NFFT
    place = np.arange(total).astype(np.float32)
    offset = (place - np.float32((total - 1) / 2.0)) / np.float32(NFFT)
    arg = np.float32(math.pi) * offset
    sinc = np.sin(arg) / arg
    window = np.float32(0.54) - np.float32(0.46) * np.cos(
        np.float32(2.0 * math.pi) * place / np.float32(total - 1)
    )
    return (sinc * window).astype(np.float32).reshape(TAPS, NFFT)[:, sample_order()]


def transform_table(devices):
    per = CHANNELS // devices
    slots = np.array([per if slot == 0 else slot for slot in SLOTS])
    channel = (per * np.arange(devices // 2)[:, None] + slots[None, :]).reshape(-1)
    channel = np.concatenate([np.zeros(EXTRA // 2, np.int64), channel])
    phase = (channel[:, None] * sample_order()[None, :] % NFFT).astype(np.float32)
    phase = phase * np.float32(2.0 * math.pi / NFFT)
    factor = np.float32((8.0 * NFFT) ** (-0.5))
    pair = np.stack([np.cos(phase) * factor, -np.sin(phase) * factor], axis=1)
    return pair.reshape(-1, NFFT).astype(ml_dtypes.bfloat16)


def separate(left, right):
    lane = lax.broadcasted_iota(jnp.int32, left.shape, 1)
    low = lane < LANES // 2
    even_first = jnp.where(low, 2 * lane, 2 * lane - LANES + 1)
    odd_first = jnp.where(low, 2 * lane + 1, 2 * lane - LANES)
    left = jnp.take_along_axis(left, even_first, axis=1, mode="promise_in_bounds")
    right = jnp.take_along_axis(right, odd_first, axis=1, mode="promise_in_bounds")
    return jnp.where(low, left, right), jnp.where(low, right, left)


def frame_part(ref, part, frame, chunk):
    both = []
    for side in range(2):
        start = frame * NFFT + (2 * chunk + side) * LANES
        both.append(ref[part, start : start + LANES].astype(jnp.float32))
    return separate(*both)


def filter_chunk(ref, first, frames, taper_ref, out_ref, chunk, past, keep=None):
    rows = ref.shape[0]
    lanes = [slice(side * HALF + chunk * LANES, side * HALF + (chunk + 1) * LANES) for side in range(2)]
    taper = [[taper_ref[tap : tap + 1, lane] for tap in range(TAPS)] for lane in lanes]
    for row in range(0, rows, 16):
        part = slice(row, row + 16)
        x = [past(t, part, chunk) for t in range(HALO)]
        for k in range(frames):
            x.append(frame_part(ref, part, first + k, chunk))
            for side in range(2):
                value = taper[side][0] * x[k][side]
                for tap in range(1, TAPS):
                    value = value + taper[side][tap] * x[k + tap][side]
                place = (first + k) % GROUP * rows + row
                out_ref[place : place + 16, lanes[side]] = value.astype(jnp.bfloat16)
        if keep is not None:
            for t in range(HALO):
                keep(t, part, chunk, x[frames + t])


def transform_part(table_ref, filtered_ref, plus_ref, minus_ref, first, count):
    even, odd = (
        product(table_ref[first : first + count, lanes], filtered_ref[:, lanes])
        for lanes in (slice(0, HALF), slice(HALF, NFFT))
    )
    row = lax.broadcasted_iota(jnp.int32, (count, LANES), 0)
    sign = jnp.where(row % 2 == 0, 1.0, -1.0)
    total = even.shape[1] // LANES
    for j in range(total):
        e, o = (value[:, j * LANES : (j + 1) * LANES] for value in (even, odd))
        plus_ref[pl.ds(first * total + j, count, stride=total), :] = e + o
        minus_ref[pl.ds(first * total + j, count, stride=total), :] = sign * (e - o)


def pack(plus_ref, minus_ref, out_ref):
    devices, pairs, sub, _ = out_ref.shape
    rows = pairs * sub
    half = devices // 2
    upper = plus_ref[rows:, :].reshape(half, pairs, sub, LANES)
    for p in range(1, pairs):
        out_ref[:half, p] = upper[:, p].astype(jnp.bfloat16)
    before = plus_ref[: half * rows, :].reshape(half, pairs, sub, LANES)[:, 0]
    place = lax.broadcasted_iota(jnp.int32, before.shape, 1)
    out_ref[:half, 0] = jnp.where(place < sub // PAIR, before, upper[:, 0]).astype(jnp.bfloat16)
    for d in range(half):
        tile = minus_ref[(d + 1) * rows : (d + 2) * rows, :]
        out_ref[devices - 1 - d] = tile.astype(jnp.bfloat16).reshape(pairs, sub, LANES)


def head_kernel(
    samples_ref, taper_ref, table_ref, out_ref, first_ref,
    held_ref, fixed_ref, carry_ref, filtered0_ref, filtered1_ref, plus_ref, minus_ref,
    packed0_ref, packed1_ref, in_sems, table_sem, out_sems, first_sem,
):
    groups = held_ref.shape[0]
    rows = samples_ref.shape[0]
    filtered, packed = (filtered0_ref, filtered1_ref), (packed0_ref, packed1_ref)
    width = GROUP * NFFT

    def fetch(g):
        source = samples_ref.at[:, pl.ds(g * width, width)]
        return pltpu.make_async_copy(source, held_ref.at[g], in_sems.at[g])

    def send(g):
        return pltpu.make_async_copy(packed[g % 2], out_ref.at[:, :, g], out_sems.at[g % 2])

    table = pltpu.make_async_copy(table_ref, fixed_ref, table_sem)
    fetch(0).start()
    fetch(1).start()
    table.start()
    for g in range(2, groups):
        fetch(g).start()

    def past(t, part, chunk):
        lane = 2 * t * HALF + chunk * LANES
        return tuple(carry_ref[part, lane + s * HALF : lane + s * HALF + LANES] for s in range(2))

    def keep(t, part, chunk, value):
        lane = 2 * t * HALF + chunk * LANES
        for s in range(2):
            carry_ref[part, lane + s * HALF : lane + s * HALF + LANES] = value[s]

    def past_in(t, part, chunk):
        return frame_part(held_ref.at[0], part, GROUP - HALO + t, chunk)

    def past_own(t, part, chunk):
        return frame_part(held_ref.at[0], part, t, chunk)

    chunks = HALF // LANES
    fetch(0).wait()
    fetch(1).wait()
    for chunk in range(chunks):
        filter_chunk(held_ref.at[1], 0, GROUP, taper_ref, filtered[1], chunk, past_in, keep)
    table.wait()
    for g in range(1, groups):
        if g > 2:
            send(g - 2).wait()
        if g + 1 < groups:
            fetch(g + 1).wait()
        first = 0
        for i, count in enumerate(PARTS):
            transform_part(fixed_ref, filtered[g % 2], plus_ref, minus_ref, first, count)
            first += count
            share = chunks // len(PARTS)
            for chunk in range(i * share, (i + 1) * share):
                if g + 1 < groups:
                    filter_chunk(
                        held_ref.at[g + 1], 0, GROUP, taper_ref, filtered[(g + 1) % 2], chunk,
                        past, keep,
                    )
                else:
                    filter_chunk(
                        held_ref.at[0], HALO, GROUP - HALO, taper_ref, filtered[(g + 1) % 2], chunk,
                        past_own,
                    )
        pack(plus_ref, minus_ref, packed[g % 2])
        send(g).start()
    kept = pl.ds(HALO * rows, (GROUP - HALO) * rows)
    last = pltpu.make_async_copy(filtered[groups % 2].at[kept], first_ref, first_sem)
    last.start()
    last.wait()
    send(groups - 2).wait()
    send(groups - 1).wait()


def head(samples, taper, table, devices):
    rows, length = samples.shape
    groups = length // (GROUP * NFFT)
    pairs = CHANNELS // devices // PAIR
    width = GROUP * rows
    sub = 2 * PAIR * width // LANES
    spectra = (devices, pairs, groups, sub, LANES)
    packed = pltpu.VMEM((devices, pairs, sub, LANES), jnp.bfloat16)
    filtered = pltpu.VMEM((width, NFFT), jnp.bfloat16)
    turned = pltpu.VMEM((table.shape[0] * width // LANES, LANES), jnp.float32)
    return pl.pallas_call(
        head_kernel,
        in_specs=[
            pl.BlockSpec(memory_space=pltpu.HBM),
            pl.BlockSpec(memory_space=pltpu.VMEM),
            pl.BlockSpec(memory_space=pltpu.HBM),
        ],
        out_specs=[
            pl.BlockSpec(memory_space=pltpu.HBM),
            pl.BlockSpec(memory_space=pltpu.HBM),
        ],
        out_shape=[
            jax.ShapeDtypeStruct(spectra, jnp.bfloat16),
            jax.ShapeDtypeStruct(((GROUP - HALO) * rows, NFFT), jnp.bfloat16),
        ],
        scratch_shapes=[
            pltpu.VMEM((groups, rows, GROUP * NFFT), jnp.int32),
            pltpu.VMEM(table.shape, jnp.bfloat16),
            pltpu.VMEM((rows, HALO * NFFT), jnp.float32),
            filtered, filtered, turned, turned, packed, packed,
            pltpu.SemaphoreType.DMA((groups,)),
            pltpu.SemaphoreType.DMA,
            pltpu.SemaphoreType.DMA((2,)),
            pltpu.SemaphoreType.DMA,
        ],
        compiler_params=pltpu.CompilerParams(vmem_limit_bytes=60 * MIB),
        cost_estimate=pl.CostEstimate(
            flops=2 * table.shape[0] * NFFT * width * 3,
            bytes_accessed=2 * table.shape[0] * NFFT + 4 * rows * length,
            transcendentals=0,
        ),
        name="head",
    )(samples, taper, table)


def tail_kernel(
    samples_ref, halo_ref, first_ref, taper_ref, table_ref, _, out_ref,
    held_ref, halo_held_ref, fixed_ref, filtered_ref, plus_ref, minus_ref, packed_ref,
    in_sems, table_sems, out_sem,
):
    rows = samples_ref.shape[0]
    kept = pl.ds(HALO * rows, (GROUP - HALO) * rows)
    begin = samples_ref.at[:, pl.ds(0, HALO * NFFT)]
    copies = [
        pltpu.make_async_copy(begin, held_ref, in_sems.at[0]),
        pltpu.make_async_copy(halo_ref, halo_held_ref, in_sems.at[1]),
        pltpu.make_async_copy(first_ref, filtered_ref.at[kept], in_sems.at[2]),
    ]
    tables = []
    first = 0
    for i, count in enumerate(PARTS):
        part = pl.ds(first, count)
        tables.append(
            pltpu.make_async_copy(table_ref.at[part], fixed_ref.at[part], table_sems.at[i])
        )
        first += count
    for copy in copies + tables:
        copy.start()

    def past(t, part, chunk):
        return frame_part(halo_held_ref, part, t, chunk)

    copies[0].wait()
    copies[1].wait()
    for chunk in range(HALF // LANES):
        filter_chunk(held_ref, 0, HALO, taper_ref, filtered_ref, chunk, past)
    copies[2].wait()
    first = 0
    for i, count in enumerate(PARTS):
        tables[i].wait()
        transform_part(fixed_ref, filtered_ref, plus_ref, minus_ref, first, count)
        first += count
    pack(plus_ref, minus_ref, packed_ref)
    send = pltpu.make_async_copy(packed_ref, out_ref.at[:, :, 0], out_sem)
    send.start()
    send.wait()


def tail(samples, halo, first, taper, table, spectra):
    rows = samples.shape[0]
    width = GROUP * rows
    devices, pairs, groups, sub, _ = spectra.shape
    turned = pltpu.VMEM((table.shape[0] * width // LANES, LANES), jnp.float32)
    return pl.pallas_call(
        tail_kernel,
        in_specs=[
            pl.BlockSpec(memory_space=pltpu.HBM),
            pl.BlockSpec(memory_space=pl.ANY),
            pl.BlockSpec(memory_space=pltpu.HBM),
            pl.BlockSpec(memory_space=pltpu.VMEM),
            pl.BlockSpec(memory_space=pltpu.HBM),
            pl.BlockSpec(memory_space=pltpu.HBM),
        ],
        out_specs=pl.BlockSpec(memory_space=pltpu.HBM),
        out_shape=jax.ShapeDtypeStruct(spectra.shape, spectra.dtype),
        scratch_shapes=[
            pltpu.VMEM((rows, HALO * NFFT), jnp.int32),
            pltpu.VMEM((rows, HALO * NFFT), jnp.bfloat16),
            pltpu.VMEM(table.shape, jnp.bfloat16),
            pltpu.VMEM((width, NFFT), jnp.bfloat16),
            turned, turned,
            pltpu.VMEM((devices, pairs, sub, LANES), jnp.bfloat16),
            pltpu.SemaphoreType.DMA((3,)),
            pltpu.SemaphoreType.DMA((len(PARTS),)),
            pltpu.SemaphoreType.DMA,
        ],
        input_output_aliases={5: 0},
        compiler_params=pltpu.CompilerParams(vmem_limit_bytes=60 * MIB),
        cost_estimate=pl.CostEstimate(
            flops=2 * table.shape[0] * NFFT * width,
            bytes_accessed=2 * table.shape[0] * NFFT,
            transcendentals=0,
        ),
        name="tail",
    )(samples, halo, first, taper, table, spectra)


def lane_turn(parts, block):
    lane = lax.broadcasted_iota(jnp.int32, parts[0].shape, 1)
    for step in (2, 1):
        upper = (lane // (block * step)) % 2 == 1
        turned = list(parts)
        for p in range(4):
            if p & step:
                continue
            low, high = parts[p], parts[p + step]
            turned[p] = jnp.where(upper, pltpu.roll(high, step * block, 1), low)
            turned[p + step] = jnp.where(upper, high, pltpu.roll(low, LANES - step * block, 1))
        parts = turned
    return parts


def spread(x, wide_ref):
    wide_ref[...] = x.astype(jnp.float32).reshape(wide_ref.shape)


def arrange(wide_ref, turned_ref, channel, feeds):
    each = wide_ref.shape[0] // feeds
    high = each // 8
    block = turned_ref.shape[1] // feeds
    inner = LANES // block
    half = turned_ref.shape[0] // 2
    for first in range(0, feeds, inner):
        for r in range(2):
            parts = []
            for f in range(first, first + inner):
                start = f * each + 4 * channel + 2 * r
                both = [wide_ref[pl.ds(start + j, high, stride=8), :] for j in range(2)]
                parts.append(jnp.concatenate(both, axis=0).astype(jnp.bfloat16))
            for k, side in enumerate(lane_turn(parts, block)):
                row = r * half + 2 * k * high
                turned_ref[row : row + 2 * high, first * block : (first + inner) * block] = side


def product(a, b):
    return lax.dot_general(a, b, (((1,), (1,)), ((), ())), preferred_element_type=jnp.float32)


def order(turned_ref, place_ref, z_ref):
    inputs = place_ref.shape[0]
    frames = turned_ref.shape[0] // 2
    z = product(place_ref[...], turned_ref[...])
    z_ref[:inputs] = z.astype(jnp.bfloat16)
    z_ref[inputs:, :frames] = z[:, frames:].astype(jnp.bfloat16)
    z_ref[inputs:, frames:] = (-z[:, :frames]).astype(jnp.bfloat16)


def correlate(z_ref, out_ref, norm):
    inputs = z_ref.shape[1]
    value = norm * product(z_ref[...], z_ref[:inputs])
    out_ref[0] = value[:inputs]
    out_ref[1] = value[inputs:]


def gram_kernel(
    feeds, norm, upper_ref, x_ref, place_ref, out_ref, held_ref, wide_ref, turned0_ref, turned1_ref,
    z0_ref, z1_ref, done0_ref, done1_ref, in_sems, out_sems,
):
    turned, z, done = (turned0_ref, turned1_ref), (z0_ref, z1_ref), (done0_ref, done1_ref)
    pairs = x_ref.shape[1]

    def fetch(pair):
        return pltpu.make_async_copy(x_ref.at[:, pair], held_ref.at[pair], in_sems.at[pair])

    def send(pair, parity):
        low, high = (pair, PAIR * pairs - pair)
        first = upper_ref[0] == parity
        local = jnp.where(pair == 0, parity * pairs, jnp.where(first, low, high))
        return pltpu.make_async_copy(done[parity], out_ref.at[local], out_sems.at[parity])

    def phase(pair, parity, third=True, second=True, first=True, wait=True):
        if first and parity == 0:
            fetch(pair).wait()
        if third:
            if wait:
                send(pair - 2, parity).wait()
            correlate(z[parity], done[parity], norm)
        if second:
            order(turned[1 - parity], place_ref, z[1 - parity])
        if first:
            if parity == 0:
                spread(held_ref[pair], wide_ref)
            arrange(wide_ref, turned[parity], parity, feeds)
        if third:
            send(pair - 1, parity).start()

    for pair in range(pairs):
        fetch(pair).start()
    phase(0, 0, third=False, second=False)
    phase(0, 1, third=False)
    phase(1, 0, wait=False)
    phase(1, 1, wait=False)

    def body(pair, _):
        phase(pair, 0)
        phase(pair, 1)
        return 0

    lax.fori_loop(2, pairs, body, 0)
    phase(pairs, 0, first=False)
    phase(pairs, 1, second=False, first=False)
    for parity in range(PAIR):
        send(pairs - 1, parity).wait()


def grams(upper, incoming, place, feeds):
    devices, pairs, groups, sub, _ = incoming.shape
    channels = PAIR * pairs
    inputs = place.shape[0]
    frames = devices * groups * sub * LANES // (2 * PAIR * inputs)
    return pl.pallas_call(
        functools.partial(gram_kernel, feeds, 1.0 / math.sqrt(frames)),
        in_specs=[
            pl.BlockSpec(memory_space=pltpu.SMEM),
            pl.BlockSpec(memory_space=pl.ANY),
            pl.BlockSpec(memory_space=pltpu.VMEM),
        ],
        out_specs=pl.BlockSpec(memory_space=pl.ANY),
        out_shape=jax.ShapeDtypeStruct((channels, 2, inputs, inputs), jnp.float32),
        scratch_shapes=[
            pltpu.VMEM((pairs, devices, groups, sub, LANES), jnp.bfloat16),
            pltpu.VMEM((devices * groups * sub, LANES), jnp.float32),
            pltpu.VMEM((2 * frames, inputs), jnp.bfloat16),
            pltpu.VMEM((2 * frames, inputs), jnp.bfloat16),
            pltpu.VMEM((2 * inputs, 2 * frames), jnp.bfloat16),
            pltpu.VMEM((2 * inputs, 2 * frames), jnp.bfloat16),
            pltpu.VMEM((2, inputs, inputs), jnp.float32),
            pltpu.VMEM((2, inputs, inputs), jnp.float32),
            pltpu.SemaphoreType.DMA((pairs,)),
            pltpu.SemaphoreType.DMA((PAIR,)),
        ],
        compiler_params=pltpu.CompilerParams(vmem_limit_bytes=60 * MIB),
        cost_estimate=pl.CostEstimate(
            flops=channels * 12 * inputs * inputs * frames,
            bytes_accessed=channels * (8 * inputs * inputs + 4 * inputs * frames),
            transcendentals=0,
        ),
        name="gram",
    )(upper, incoming, place)


def per_device(samples, input_map):
    feeds = lax.axis_size("feed")
    times = lax.axis_size("tm")
    devices = feeds * times
    inputs = input_map.shape[0]
    taper = jnp.asarray(taper_table())
    table = jnp.asarray(transform_table(devices))
    last = samples[:, samples.shape[1] - HALO * NFFT :].astype(jnp.bfloat16)
    halo = lax.ppermute(last, "tm", [(t, t + 1) for t in range(times - 1)])
    place = (input_map[:, None] == jnp.arange(inputs)[None, :]).astype(jnp.bfloat16)
    device = lax.axis_index("feed") * times + lax.axis_index("tm")
    upper = (2 * device // devices).astype(jnp.int32).reshape(1)
    spectra, first = head(samples, taper, table, devices)
    outgoing = tail(samples, halo, first, taper, table, spectra)
    incoming = lax.all_to_all(outgoing, ("feed", "tm"), split_axis=0, concat_axis=0, tiled=True)
    return grams(upper, incoming, place, feeds)


def solution(mesh):
    in_specs = (P("feed", "tm"), P())
    out_specs = P(("feed", "tm"), None, None, None)
    return jax.shard_map(
        per_device, mesh=mesh, in_specs=in_specs, out_specs=out_specs, check_vma=False
    )
```

```python
import functools
import math

import jax
import jax.numpy as jnp
import ml_dtypes
import numpy as np
from jax import lax
from jax.experimental import pallas as pl
from jax.experimental.pallas import tpu as pltpu
from jax.sharding import PartitionSpec as P

CHANNELS = 1024
NFFT = 2048
HALF = NFFT // 2
TAPS = 4
HALO = TAPS - 1
LANES = 128
GROUP = 8
PAIR = 2
SLOTS = (0, 4, 1, 7, 2, 6, 3, 5)
EXTRA = 16
PARTS = (528, 512)
MIB = 1024 * 1024


def sample_order():
    chunk = 2 * LANES * np.arange(HALF // LANES)[:, None]
    lane = np.arange(LANES)[None, :]
    even = chunk + 2 * lane
    odd = chunk + (LANES + 2 * lane) % (2 * LANES) + 1
    return np.concatenate([even.reshape(-1), odd.reshape(-1)])


def taper_table():
    total = TAPS * NFFT
    place = np.arange(total).astype(np.float32)
    offset = (place - np.float32((total - 1) / 2.0)) / np.float32(NFFT)
    arg = np.float32(math.pi) * offset
    sinc = np.sin(arg) / arg
    window = np.float32(0.54) - np.float32(0.46) * np.cos(
        np.float32(2.0 * math.pi) * place / np.float32(total - 1)
    )
    return (sinc * window).astype(np.float32).reshape(TAPS, NFFT)[:, sample_order()]


def transform_table(devices):
    per = CHANNELS // devices
    slots = np.array([per if slot == 0 else slot for slot in SLOTS])
    channel = (per * np.arange(devices // 2)[:, None] + slots[None, :]).reshape(-1)
    channel = np.concatenate([np.zeros(EXTRA // 2, np.int64), channel])
    phase = (channel[:, None] * sample_order()[None, :] % NFFT).astype(np.float32)
    phase = phase * np.float32(2.0 * math.pi / NFFT)
    factor = np.float32((8.0 * NFFT) ** (-0.5))
    pair = np.stack([np.cos(phase) * factor, -np.sin(phase) * factor], axis=1)
    return pair.reshape(-1, NFFT).astype(ml_dtypes.bfloat16)


def separate(left, right):
    lane = lax.broadcasted_iota(jnp.int32, left.shape, 1)
    low = lane < LANES // 2
    even_first = jnp.where(low, 2 * lane, 2 * lane - LANES + 1)
    odd_first = jnp.where(low, 2 * lane + 1, 2 * lane - LANES)
    left = jnp.take_along_axis(left, even_first, axis=1, mode="promise_in_bounds")
    right = jnp.take_along_axis(right, odd_first, axis=1, mode="promise_in_bounds")
    return jnp.where(low, left, right), jnp.where(low, right, left)


def frame_part(ref, part, frame, chunk):
    both = []
    for side in range(2):
        start = frame * NFFT + (2 * chunk + side) * LANES
        both.append(ref[part, start : start + LANES].astype(jnp.float32))
    return separate(*both)


def filter_chunk(ref, frames, taper_ref, out_ref, place, chunk, past, keep=None):
    rows = ref.shape[0]
    lanes = [slice(side * HALF + chunk * LANES, side * HALF + (chunk + 1) * LANES) for side in range(2)]
    taper = [[taper_ref[tap : tap + 1, lane] for tap in range(TAPS)] for lane in lanes]
    for row in range(0, rows, 16):
        part = slice(row, row + 16)
        x = [past(t, part, chunk) for t in range(HALO)]
        for k in range(frames):
            x.append(frame_part(ref, part, k, chunk))
            for side in range(2):
                value = taper[side][0] * x[k][side]
                for tap in range(1, TAPS):
                    value = value + taper[side][tap] * x[k + tap][side]
                start = (place + k) * rows + row
                out_ref[start : start + 16, lanes[side]] = value.astype(jnp.bfloat16)
        if keep is not None:
            for t in range(HALO):
                keep(t, part, chunk, x[frames + t])


def transform_part(table_ref, filtered_ref, plus_ref, minus_ref, first, count):
    even, odd = (
        product(table_ref[first : first + count, lanes], filtered_ref[:, lanes])
        for lanes in (slice(0, HALF), slice(HALF, NFFT))
    )
    row = lax.broadcasted_iota(jnp.int32, (count, LANES), 0)
    sign = jnp.where(row % 2 == 0, 1.0, -1.0)
    total = even.shape[1] // LANES
    for j in range(total):
        e, o = (value[:, j * LANES : (j + 1) * LANES] for value in (even, odd))
        plus_ref[pl.ds(first * total + j, count, stride=total), :] = e + o
        minus_ref[pl.ds(first * total + j, count, stride=total), :] = sign * (e - o)


def pack_lower(plus_ref, out_ref):
    devices, pairs, sub, _ = out_ref.shape
    rows = pairs * sub
    half = devices // 2
    upper = plus_ref[rows:, :].reshape(half, pairs, sub, LANES)
    for p in range(1, pairs):
        out_ref[:half, p] = upper[:, p].astype(jnp.bfloat16)
    before = plus_ref[: half * rows, :].reshape(half, pairs, sub, LANES)[:, 0]
    place = lax.broadcasted_iota(jnp.int32, before.shape, 1)
    out_ref[:half, 0] = jnp.where(place < sub // PAIR, before, upper[:, 0]).astype(jnp.bfloat16)


def pack_upper(minus_ref, out_ref):
    devices, pairs, sub, _ = out_ref.shape
    rows = pairs * sub
    for d in range(devices // 2):
        tile = minus_ref[(d + 1) * rows : (d + 2) * rows, :]
        out_ref[devices - 1 - d] = tile.astype(jnp.bfloat16).reshape(pairs, sub, LANES)


def head_kernel(
    samples_ref, curve_ref, table_ref, out_ref, first_ref, begin_ref, taper_ref, fixed_ref,
    rest_ref, held_ref, carry_ref, filtered0_ref, filtered1_ref, plus0_ref, plus1_ref,
    minus0_ref, minus1_ref, packed0_ref, packed1_ref, in_sems, out_sems,
):
    groups = held_ref.shape[0] + 1
    filtered, packed = (filtered0_ref, filtered1_ref), (packed0_ref, packed1_ref)
    plus, minus = (plus0_ref, plus1_ref), (minus0_ref, minus1_ref)
    width = GROUP * NFFT

    def fetch(g):
        source = samples_ref.at[:, pl.ds(g * width, width)]
        return pltpu.make_async_copy(source, held_ref.at[g - 1], in_sems.at[g])

    def send(g):
        return pltpu.make_async_copy(packed[g % 2], out_ref.at[:, :, g], out_sems.at[g % 2])

    begin = pltpu.make_async_copy(
        samples_ref.at[:, pl.ds(0, HALO * NFFT)], begin_ref, in_sems.at[0]
    )
    rest = pltpu.make_async_copy(
        samples_ref.at[:, pl.ds(HALO * NFFT, (GROUP - HALO) * NFFT)], rest_ref, in_sems.at[groups]
    )
    table = pltpu.make_async_copy(table_ref, fixed_ref, in_sems.at[groups + 1])
    taper = pltpu.make_async_copy(curve_ref, taper_ref, in_sems.at[groups + 2])
    taper.start()
    rest.start()
    fetch(1).start()
    table.start()
    for g in range(2, groups):
        fetch(g).start()
    begin.start()

    def past(t, part, chunk):
        lane = 2 * t * HALF + chunk * LANES
        return tuple(carry_ref[part, lane + s * HALF : lane + s * HALF + LANES] for s in range(2))

    def keep(t, part, chunk, value):
        lane = 2 * t * HALF + chunk * LANES
        for s in range(2):
            carry_ref[part, lane + s * HALF : lane + s * HALF + LANES] = value[s]

    def past_in(t, part, chunk):
        return frame_part(rest_ref, part, GROUP - 2 * HALO + t, chunk)

    def past_own(t, part, chunk):
        return frame_part(begin_ref, part, t, chunk)

    chunks = HALF // LANES
    taper.wait()
    rest.wait()
    fetch(1).wait()
    for chunk in range(chunks):
        filter_chunk(held_ref.at[0], GROUP, taper_ref, filtered[1], 0, chunk, past_in, keep)
    table.wait()
    for g in range(1, groups):
        now = g % 2
        if g + 1 < groups:
            fetch(g + 1).wait()
        else:
            begin.wait()
        if g > 3:
            send(g - 3).wait()
        first = 0
        for i, count in enumerate(PARTS):
            transform_part(fixed_ref, filtered[now], plus[now], minus[now], first, count)
            first += count
            if g > 1:
                if i == 0:
                    pack_lower(plus[1 - now], packed[1 - now])
                if i == len(PARTS) - 1:
                    pack_upper(minus[1 - now], packed[1 - now])
            share = chunks // len(PARTS)
            for chunk in range(i * share, (i + 1) * share):
                if g + 1 < groups:
                    filter_chunk(
                        held_ref.at[g], GROUP, taper_ref, filtered[1 - now], 0, chunk, past, keep
                    )
                else:
                    filter_chunk(
                        rest_ref, GROUP - HALO, taper_ref, first_ref, HALO, chunk, past_own
                    )
        if g > 1:
            send(g - 1).start()
    last = (groups - 1) % 2
    send(groups - 3).wait()
    pack_lower(plus[last], packed[last])
    pack_upper(minus[last], packed[last])
    send(groups - 1).start()
    send(groups - 2).wait()
    send(groups - 1).wait()


def in_hbm(*values):
    return tuple(pltpu.with_memory_space_constraint(value, pltpu.HBM) for value in values)


def in_vmem(*values):
    return tuple(pltpu.with_memory_space_constraint(value, pltpu.VMEM) for value in values)


def head(samples, taper, table, devices):
    rows, length = samples.shape
    groups = length // (GROUP * NFFT)
    pairs = CHANNELS // devices // PAIR
    width = GROUP * rows
    sub = 2 * PAIR * width // LANES
    spectra = (devices, pairs, groups, sub, LANES)
    packed = pltpu.VMEM((devices, pairs, sub, LANES), jnp.bfloat16)
    filtered = pltpu.VMEM((width, NFFT), jnp.bfloat16)
    turned = pltpu.VMEM((table.shape[0] * width // LANES, LANES), jnp.float32)
    return pl.pallas_call(
        head_kernel,
        in_specs=[
            pl.BlockSpec(memory_space=pltpu.HBM),
            pl.BlockSpec(memory_space=pltpu.HBM),
            pl.BlockSpec(memory_space=pltpu.HBM),
        ],
        out_specs=[pl.BlockSpec(memory_space=pltpu.HBM)]
        + [pl.BlockSpec(memory_space=pltpu.VMEM)] * 4,
        out_shape=[
            pltpu.HBM(spectra, jnp.bfloat16),
            pltpu.VMEM((width, NFFT), jnp.bfloat16),
            pltpu.VMEM((rows, HALO * NFFT), jnp.int32),
            pltpu.VMEM(taper.shape, jnp.float32),
            pltpu.VMEM(table.shape, jnp.bfloat16),
        ],
        scratch_shapes=[
            pltpu.VMEM((rows, (GROUP - HALO) * NFFT), jnp.int32),
            pltpu.VMEM((groups - 1, rows, GROUP * NFFT), jnp.int32),
            pltpu.VMEM((rows, HALO * NFFT), jnp.float32),
            filtered, filtered, turned, turned, turned, turned, packed, packed,
            pltpu.SemaphoreType.DMA((groups + 3,)),
            pltpu.SemaphoreType.DMA((2,)),
        ],
        compiler_params=pltpu.CompilerParams(vmem_limit_bytes=40 * MIB),
        cost_estimate=pl.CostEstimate(
            flops=2 * table.shape[0] * NFFT * width * 3,
            bytes_accessed=2 * table.shape[0] * NFFT + 4 * rows * length,
            transcendentals=0,
        ),
        name="head",
    )(*in_hbm(samples, taper, table))


def tail_kernel(
    begin_ref, halo_ref, first_ref, taper_ref, fixed_ref, _, out_ref,
    filtered_ref, plus_ref, minus_ref, packed_ref, out_sems,
):
    rows = begin_ref.shape[0]
    kept = HALO * rows
    half = packed_ref.shape[0] // 2

    def past(t, part, chunk):
        return frame_part(halo_ref, part, t, chunk)

    def send(side):
        part = pl.ds(side * half, half)
        return pltpu.make_async_copy(packed_ref.at[part], out_ref.at[part, :, 0], out_sems.at[side])

    filtered_ref[kept:, :] = first_ref[kept:, :]
    for chunk in range(HALF // LANES):
        filter_chunk(begin_ref, HALO, taper_ref, filtered_ref, 0, chunk, past)
    first = 0
    for count in PARTS:
        transform_part(fixed_ref, filtered_ref, plus_ref, minus_ref, first, count)
        first += count
    pack_lower(plus_ref, packed_ref)
    send(0).start()
    pack_upper(minus_ref, packed_ref)
    send(1).start()
    send(0).wait()
    send(1).wait()


def tail(begin, halo, first, taper, fixed, spectra):
    rows = begin.shape[0]
    width = GROUP * rows
    devices, pairs, _, sub, _ = spectra.shape
    turned = pltpu.VMEM((fixed.shape[0] * width // LANES, LANES), jnp.float32)
    return pl.pallas_call(
        tail_kernel,
        in_specs=[pl.BlockSpec(memory_space=pltpu.VMEM)] * 5
        + [pl.BlockSpec(memory_space=pltpu.HBM)],
        out_specs=pl.BlockSpec(memory_space=pltpu.HBM),
        out_shape=pltpu.HBM(spectra.shape, spectra.dtype),
        scratch_shapes=[
            pltpu.VMEM((width, NFFT), jnp.bfloat16),
            turned, turned,
            pltpu.VMEM((devices, pairs, sub, LANES), jnp.bfloat16),
            pltpu.SemaphoreType.DMA((2,)),
        ],
        input_output_aliases={5: 0},
        compiler_params=pltpu.CompilerParams(vmem_limit_bytes=32 * MIB),
        cost_estimate=pl.CostEstimate(
            flops=2 * fixed.shape[0] * NFFT * width,
            bytes_accessed=2 * fixed.shape[0] * NFFT,
            transcendentals=0,
        ),
        name="tail",
    )(*in_vmem(begin, halo, first, taper, fixed), *in_hbm(spectra))


def lane_turn(parts, block):
    lane = lax.broadcasted_iota(jnp.int32, parts[0].shape, 1)
    for step in (2, 1):
        upper = (lane // (block * step)) % 2 == 1
        turned = list(parts)
        for p in range(4):
            if p & step:
                continue
            low, high = parts[p], parts[p + step]
            turned[p] = jnp.where(upper, pltpu.roll(high, step * block, 1), low)
            turned[p + step] = jnp.where(upper, high, pltpu.roll(low, LANES - step * block, 1))
        parts = turned
    return parts


def spread(x, wide_ref):
    wide_ref[...] = x.astype(jnp.float32).reshape(wide_ref.shape)


def arrange(wide_ref, turned_ref, channel, feeds):
    each = wide_ref.shape[0] // feeds
    high = each // 8
    block = turned_ref.shape[1] // feeds
    inner = LANES // block
    half = turned_ref.shape[0] // 2
    for first in range(0, feeds, inner):
        for r in range(2):
            parts = []
            for f in range(first, first + inner):
                start = f * each + 4 * channel + 2 * r
                both = [wide_ref[pl.ds(start + j, high, stride=8), :] for j in range(2)]
                parts.append(jnp.concatenate(both, axis=0).astype(jnp.bfloat16))
            for k, side in enumerate(lane_turn(parts, block)):
                row = r * half + 2 * k * high
                turned_ref[row : row + 2 * high, first * block : (first + inner) * block] = side


def product(a, b):
    return lax.dot_general(a, b, (((1,), (1,)), ((), ())), preferred_element_type=jnp.float32)


def order(turned_ref, place_ref, z_ref):
    inputs = place_ref.shape[0]
    frames = turned_ref.shape[0] // 2
    z = product(place_ref[...], turned_ref[...])
    z_ref[:inputs] = z.astype(jnp.bfloat16)
    z_ref[inputs:, :frames] = z[:, frames:].astype(jnp.bfloat16)
    z_ref[inputs:, frames:] = (-z[:, :frames]).astype(jnp.bfloat16)


def correlate(z_ref, out_ref, norm):
    inputs = z_ref.shape[1]
    value = norm * product(z_ref[...], z_ref[:inputs])
    out_ref[0] = value[:inputs]
    out_ref[1] = value[inputs:]


def gram_kernel(
    feeds, norm, upper_ref, x_ref, place_ref, out_ref, held_ref, wide_ref, turned0_ref, turned1_ref,
    z0_ref, z1_ref, done0_ref, done1_ref, in_sems, out_sems,
):
    turned, z, done = (turned0_ref, turned1_ref), (z0_ref, z1_ref), (done0_ref, done1_ref)
    pairs = x_ref.shape[1]

    def fetch(pair):
        return pltpu.make_async_copy(x_ref.at[:, pair], held_ref.at[pair], in_sems.at[pair])

    def send(pair, parity):
        low, high = (pair, PAIR * pairs - pair)
        first = upper_ref[0] == parity
        local = jnp.where(pair == 0, parity * pairs, jnp.where(first, low, high))
        return pltpu.make_async_copy(done[parity], out_ref.at[local], out_sems.at[parity])

    def phase(pair, parity, third=True, second=True, first=True, wait=True, wait_more=True):
        if first and parity == 0:
            fetch(pair).wait()
            if not wait_more:
                for later in range(1, pairs):
                    fetch(later).start()
        if third:
            if wait:
                send(pair - 2, parity).wait()
            correlate(z[parity], done[parity], norm)
        if second:
            order(turned[1 - parity], place_ref, z[1 - parity])
        if first:
            if parity == 0:
                spread(held_ref[pair], wide_ref)
            arrange(wide_ref, turned[parity], parity, feeds)
        if third:
            send(pair - 1, parity).start()

    fetch(0).start()
    phase(0, 0, third=False, second=False, wait_more=False)
    phase(0, 1, third=False)
    phase(1, 0, wait=False)
    phase(1, 1, wait=False)

    def body(pair, _):
        phase(pair, 0)
        phase(pair, 1)
        return 0

    lax.fori_loop(2, pairs, body, 0)
    phase(pairs, 0, first=False)
    phase(pairs, 1, second=False, first=False)
    for parity in range(PAIR):
        send(pairs - 1, parity).wait()


def grams(upper, incoming, place, feeds):
    devices, pairs, groups, sub, _ = incoming.shape
    channels = PAIR * pairs
    inputs = place.shape[0]
    frames = devices * groups * sub * LANES // (2 * PAIR * inputs)
    return pl.pallas_call(
        functools.partial(gram_kernel, feeds, 1.0 / math.sqrt(frames)),
        in_specs=[
            pl.BlockSpec(memory_space=pltpu.SMEM),
            pl.BlockSpec(memory_space=pl.ANY),
            pl.BlockSpec(memory_space=pltpu.VMEM),
        ],
        out_specs=pl.BlockSpec(memory_space=pl.ANY),
        out_shape=jax.ShapeDtypeStruct((channels, 2, inputs, inputs), jnp.float32),
        scratch_shapes=[
            pltpu.VMEM((pairs, devices, groups, sub, LANES), jnp.bfloat16),
            pltpu.VMEM((devices * groups * sub, LANES), jnp.float32),
            pltpu.VMEM((2 * frames, inputs), jnp.bfloat16),
            pltpu.VMEM((2 * frames, inputs), jnp.bfloat16),
            pltpu.VMEM((2 * inputs, 2 * frames), jnp.bfloat16),
            pltpu.VMEM((2 * inputs, 2 * frames), jnp.bfloat16),
            pltpu.VMEM((2, inputs, inputs), jnp.float32),
            pltpu.VMEM((2, inputs, inputs), jnp.float32),
            pltpu.SemaphoreType.DMA((pairs,)),
            pltpu.SemaphoreType.DMA((PAIR,)),
        ],
        compiler_params=pltpu.CompilerParams(vmem_limit_bytes=40 * MIB),
        cost_estimate=pl.CostEstimate(
            flops=channels * 12 * inputs * inputs * frames,
            bytes_accessed=channels * (8 * inputs * inputs + 4 * inputs * frames),
            transcendentals=0,
        ),
        name="gram",
    )(upper, *in_hbm(incoming), place)


def per_device(samples, input_map):
    feeds = lax.axis_size("feed")
    times = lax.axis_size("tm")
    devices = feeds * times
    inputs = input_map.shape[0]
    taper = jnp.asarray(taper_table())
    table = jnp.asarray(transform_table(devices))
    last = samples[:, samples.shape[1] - HALO * NFFT :].astype(jnp.bfloat16)
    halo = lax.ppermute(last, "tm", [(t, t + 1) for t in range(times - 1)])
    place = (input_map[:, None] == jnp.arange(inputs)[None, :]).astype(jnp.bfloat16)
    device = lax.axis_index("feed") * times + lax.axis_index("tm")
    upper = (2 * device // devices).astype(jnp.int32).reshape(1)
    spectra, *held = head(samples, taper, table, devices)
    first, begin, curve, fixed = held
    outgoing = tail(begin, halo, first, curve, fixed, spectra)
    incoming = lax.all_to_all(outgoing, ("feed", "tm"), split_axis=0, concat_axis=0, tiled=True)
    return grams(upper, incoming, place, feeds)


def solution(mesh):
    in_specs = (P("feed", "tm"), P())
    out_specs = P(("feed", "tm"), None, None, None)
    return jax.shard_map(
        per_device, mesh=mesh, in_specs=in_specs, out_specs=out_specs, check_vma=False
    )
```

```python
import functools
import math

import jax
import jax.numpy as jnp
import ml_dtypes
import numpy as np
from jax import lax
from jax.experimental import pallas as pl
from jax.experimental.pallas import tpu as pltpu
from jax.sharding import PartitionSpec as P

CHANNELS = 1024
NFFT = 2048
HALF = NFFT // 2
TAPS = 4
HALO = TAPS - 1
LANES = 128
GROUP = 8
PAIR = 2
SLOTS = (0, 4, 1, 7, 2, 6, 3, 5)
EXTRA = 16
PARTS = (528, 512)
MIB = 1024 * 1024


def sample_order():
    chunk = 2 * LANES * np.arange(HALF // LANES)[:, None]
    lane = np.arange(LANES)[None, :]
    even = chunk + 2 * lane
    odd = chunk + (LANES + 2 * lane) % (2 * LANES) + 1
    return np.concatenate([even.reshape(-1), odd.reshape(-1)])


def taper_table():
    total = TAPS * NFFT
    place = np.arange(total).astype(np.float32)
    offset = (place - np.float32((total - 1) / 2.0)) / np.float32(NFFT)
    arg = np.float32(math.pi) * offset
    sinc = np.sin(arg) / arg
    window = np.float32(0.54) - np.float32(0.46) * np.cos(
        np.float32(2.0 * math.pi) * place / np.float32(total - 1)
    )
    return (sinc * window).astype(np.float32).reshape(TAPS, NFFT)[:, sample_order()]


def transform_table(devices):
    per = CHANNELS // devices
    slots = np.array([per if slot == 0 else slot for slot in SLOTS])
    channel = (per * np.arange(devices // 2)[:, None] + slots[None, :]).reshape(-1)
    channel = np.concatenate([np.zeros(EXTRA // 2, np.int64), channel])
    phase = (channel[:, None] * sample_order()[None, :] % NFFT).astype(np.float32)
    phase = phase * np.float32(2.0 * math.pi / NFFT)
    factor = np.float32((8.0 * NFFT) ** (-0.5))
    pair = np.stack([np.cos(phase) * factor, -np.sin(phase) * factor], axis=1)
    return pair.reshape(-1, NFFT).astype(ml_dtypes.bfloat16)


def separate(left, right):
    lane = lax.broadcasted_iota(jnp.int32, left.shape, 1)
    low = lane < LANES // 2
    even_first = jnp.where(low, 2 * lane, 2 * lane - LANES + 1)
    odd_first = jnp.where(low, 2 * lane + 1, 2 * lane - LANES)
    left = jnp.take_along_axis(left, even_first, axis=1, mode="promise_in_bounds")
    right = jnp.take_along_axis(right, odd_first, axis=1, mode="promise_in_bounds")
    return jnp.where(low, left, right), jnp.where(low, right, left)


def frame_part(ref, part, frame, chunk):
    both = []
    for side in range(2):
        start = frame * NFFT + (2 * chunk + side) * LANES
        both.append(ref[part, start : start + LANES].astype(jnp.float32))
    return separate(*both)


def filter_chunk(ref, frames, taper_ref, out_ref, place, chunk, past, keep=None):
    rows = ref.shape[0]
    lanes = [slice(side * HALF + chunk * LANES, side * HALF + (chunk + 1) * LANES) for side in range(2)]
    taper = [[taper_ref[tap : tap + 1, lane] for tap in range(TAPS)] for lane in lanes]
    for row in range(0, rows, 16):
        part = slice(row, row + 16)
        x = [past(t, part, chunk) for t in range(HALO)]
        for k in range(frames):
            x.append(frame_part(ref, part, k, chunk))
            for side in range(2):
                value = taper[side][0] * x[k][side]
                for tap in range(1, TAPS):
                    value = value + taper[side][tap] * x[k + tap][side]
                start = (place + k) * rows + row
                out_ref[start : start + 16, lanes[side]] = value.astype(jnp.bfloat16)
        if keep is not None:
            for t in range(HALO):
                keep(t, part, chunk, x[frames + t])


def transform_part(table_ref, filtered_ref, plus_ref, minus_ref, first, count):
    even, odd = (
        product(table_ref[first : first + count, lanes], filtered_ref[:, lanes])
        for lanes in (slice(0, HALF), slice(HALF, NFFT))
    )
    row = lax.broadcasted_iota(jnp.int32, (count, LANES), 0)
    sign = jnp.where(row % 2 == 0, 1.0, -1.0)
    total = even.shape[1] // LANES
    for j in range(total):
        e, o = (value[:, j * LANES : (j + 1) * LANES] for value in (even, odd))
        plus_ref[pl.ds(first * total + j, count, stride=total), :] = e + o
        minus_ref[pl.ds(first * total + j, count, stride=total), :] = sign * (e - o)


def pack_lower(plus_ref, out_ref):
    devices, pairs, sub, _ = out_ref.shape
    rows = pairs * sub
    half = devices // 2
    upper = plus_ref[rows:, :].reshape(half, pairs, sub, LANES)
    for p in range(1, pairs):
        out_ref[:half, p] = upper[:, p].astype(jnp.bfloat16)
    before = plus_ref[: half * rows, :].reshape(half, pairs, sub, LANES)[:, 0]
    place = lax.broadcasted_iota(jnp.int32, before.shape, 1)
    out_ref[:half, 0] = jnp.where(place < sub // PAIR, before, upper[:, 0]).astype(jnp.bfloat16)


def pack_upper(minus_ref, out_ref):
    devices, pairs, sub, _ = out_ref.shape
    rows = pairs * sub
    for d in range(devices // 2):
        tile = minus_ref[(d + 1) * rows : (d + 2) * rows, :]
        out_ref[devices - 1 - d] = tile.astype(jnp.bfloat16).reshape(pairs, sub, LANES)


def head_kernel(
    samples_ref, curve_ref, table_ref, out_ref, first_ref, begin_ref, taper_ref, fixed_ref,
    rest_ref, held_ref, carry_ref, filtered0_ref, filtered1_ref, plus0_ref, plus1_ref,
    minus0_ref, minus1_ref, packed0_ref, packed1_ref, in_sems, out_sems,
):
    groups = held_ref.shape[0] + 1
    filtered, packed = (filtered0_ref, filtered1_ref), (packed0_ref, packed1_ref)
    plus, minus = (plus0_ref, plus1_ref), (minus0_ref, minus1_ref)
    width = GROUP * NFFT

    def fetch(g):
        source = samples_ref.at[:, pl.ds(g * width, width)]
        return pltpu.make_async_copy(source, held_ref.at[g - 1], in_sems.at[g])

    def send(g):
        return pltpu.make_async_copy(packed[g % 2], out_ref.at[:, :, g], out_sems.at[g % 2])

    begin = pltpu.make_async_copy(
        samples_ref.at[:, pl.ds(0, HALO * NFFT)], begin_ref, in_sems.at[0]
    )
    rest = pltpu.make_async_copy(
        samples_ref.at[:, pl.ds(HALO * NFFT, (GROUP - HALO) * NFFT)], rest_ref, in_sems.at[groups]
    )
    table = pltpu.make_async_copy(table_ref, fixed_ref, in_sems.at[groups + 1])
    taper = pltpu.make_async_copy(curve_ref, taper_ref, in_sems.at[groups + 2])
    taper.start()
    rest.start()
    fetch(1).start()
    table.start()
    for g in range(2, groups):
        fetch(g).start()
    begin.start()

    def past(t, part, chunk):
        lane = 2 * t * HALF + chunk * LANES
        return tuple(carry_ref[part, lane + s * HALF : lane + s * HALF + LANES] for s in range(2))

    def keep(t, part, chunk, value):
        lane = 2 * t * HALF + chunk * LANES
        for s in range(2):
            carry_ref[part, lane + s * HALF : lane + s * HALF + LANES] = value[s]

    def past_in(t, part, chunk):
        return frame_part(rest_ref, part, GROUP - 2 * HALO + t, chunk)

    def past_own(t, part, chunk):
        return frame_part(begin_ref, part, t, chunk)

    chunks = HALF // LANES
    taper.wait()
    rest.wait()
    fetch(1).wait()
    for chunk in range(chunks):
        filter_chunk(held_ref.at[0], GROUP, taper_ref, filtered[1], 0, chunk, past_in, keep)
    table.wait()
    for g in range(1, groups):
        now = g % 2
        if g + 1 < groups:
            fetch(g + 1).wait()
        else:
            begin.wait()
        if g > 3:
            send(g - 3).wait()
        first = 0
        for i, count in enumerate(PARTS):
            transform_part(fixed_ref, filtered[now], plus[now], minus[now], first, count)
            first += count
            if g > 1:
                if i == 0:
                    pack_lower(plus[1 - now], packed[1 - now])
                if i == len(PARTS) - 1:
                    pack_upper(minus[1 - now], packed[1 - now])
            share = chunks // len(PARTS)
            for chunk in range(i * share, (i + 1) * share):
                if g + 1 < groups:
                    filter_chunk(
                        held_ref.at[g], GROUP, taper_ref, filtered[1 - now], 0, chunk, past, keep
                    )
                else:
                    filter_chunk(
                        rest_ref, GROUP - HALO, taper_ref, first_ref, HALO, chunk, past_own
                    )
        if g > 1:
            send(g - 1).start()
    last = (groups - 1) % 2
    send(groups - 3).wait()
    pack_lower(plus[last], packed[last])
    pack_upper(minus[last], packed[last])
    send(groups - 1).start()
    send(groups - 2).wait()
    send(groups - 1).wait()


def in_hbm(*values):
    return tuple(pltpu.with_memory_space_constraint(value, pltpu.HBM) for value in values)


def in_vmem(*values):
    return tuple(pltpu.with_memory_space_constraint(value, pltpu.VMEM) for value in values)


def head(samples, taper, table, devices):
    rows, length = samples.shape
    groups = length // (GROUP * NFFT)
    pairs = CHANNELS // devices // PAIR
    width = GROUP * rows
    sub = 2 * PAIR * width // LANES
    spectra = (devices, pairs, groups, sub, LANES)
    packed = pltpu.VMEM((devices, pairs, sub, LANES), jnp.bfloat16)
    filtered = pltpu.VMEM((width, NFFT), jnp.bfloat16)
    turned = pltpu.VMEM((table.shape[0] * width // LANES, LANES), jnp.float32)
    return pl.pallas_call(
        head_kernel,
        in_specs=[
            pl.BlockSpec(memory_space=pltpu.HBM),
            pl.BlockSpec(memory_space=pltpu.HBM),
            pl.BlockSpec(memory_space=pltpu.HBM),
        ],
        out_specs=[pl.BlockSpec(memory_space=pltpu.HBM)]
        + [pl.BlockSpec(memory_space=pltpu.VMEM)] * 4,
        out_shape=[
            pltpu.HBM(spectra, jnp.bfloat16),
            pltpu.VMEM((width, NFFT), jnp.bfloat16),
            pltpu.VMEM((rows, HALO * NFFT), jnp.int32),
            pltpu.VMEM(taper.shape, jnp.float32),
            pltpu.VMEM(table.shape, jnp.bfloat16),
        ],
        scratch_shapes=[
            pltpu.VMEM((rows, (GROUP - HALO) * NFFT), jnp.int32),
            pltpu.VMEM((groups - 1, rows, GROUP * NFFT), jnp.int32),
            pltpu.VMEM((rows, HALO * NFFT), jnp.float32),
            filtered, filtered, turned, turned, turned, turned, packed, packed,
            pltpu.SemaphoreType.DMA((groups + 3,)),
            pltpu.SemaphoreType.DMA((2,)),
        ],
        compiler_params=pltpu.CompilerParams(vmem_limit_bytes=40 * MIB),
        cost_estimate=pl.CostEstimate(
            flops=2 * table.shape[0] * NFFT * width * 3,
            bytes_accessed=2 * table.shape[0] * NFFT + 4 * rows * length,
            transcendentals=0,
        ),
        name="head",
    )(*in_hbm(samples, taper, table))


def tail_kernel(
    begin_ref, halo_ref, first_ref, taper_ref, fixed_ref, _, out_ref,
    filtered_ref, plus_ref, minus_ref, packed_ref, out_sems,
):
    rows = begin_ref.shape[0]
    kept = HALO * rows
    half = packed_ref.shape[0] // 2

    def past(t, part, chunk):
        return frame_part(halo_ref, part, t, chunk)

    def send(side):
        part = pl.ds(side * half, half)
        return pltpu.make_async_copy(packed_ref.at[part], out_ref.at[part, :, 0], out_sems.at[side])

    filtered_ref[kept:, :] = first_ref[kept:, :]
    for chunk in range(HALF // LANES):
        filter_chunk(begin_ref, HALO, taper_ref, filtered_ref, 0, chunk, past)
    first = 0
    for count in PARTS:
        transform_part(fixed_ref, filtered_ref, plus_ref, minus_ref, first, count)
        first += count
    pack_lower(plus_ref, packed_ref)
    send(0).start()
    pack_upper(minus_ref, packed_ref)
    send(1).start()
    send(0).wait()
    send(1).wait()


def tail(begin, halo, first, taper, fixed, spectra):
    rows = begin.shape[0]
    width = GROUP * rows
    devices, pairs, _, sub, _ = spectra.shape
    turned = pltpu.VMEM((fixed.shape[0] * width // LANES, LANES), jnp.float32)
    return pl.pallas_call(
        tail_kernel,
        in_specs=[pl.BlockSpec(memory_space=pltpu.VMEM)] * 5
        + [pl.BlockSpec(memory_space=pltpu.HBM)],
        out_specs=pl.BlockSpec(memory_space=pltpu.HBM),
        out_shape=pltpu.HBM(spectra.shape, spectra.dtype),
        scratch_shapes=[
            pltpu.VMEM((width, NFFT), jnp.bfloat16),
            turned, turned,
            pltpu.VMEM((devices, pairs, sub, LANES), jnp.bfloat16),
            pltpu.SemaphoreType.DMA((2,)),
        ],
        input_output_aliases={5: 0},
        compiler_params=pltpu.CompilerParams(vmem_limit_bytes=32 * MIB),
        cost_estimate=pl.CostEstimate(
            flops=2 * fixed.shape[0] * NFFT * width,
            bytes_accessed=2 * fixed.shape[0] * NFFT,
            transcendentals=0,
        ),
        name="tail",
    )(*in_vmem(begin, halo, first, taper, fixed), *in_hbm(spectra))


def lane_turn(parts, block):
    lane = lax.broadcasted_iota(jnp.int32, parts[0].shape, 1)
    for step in (2, 1):
        upper = (lane // (block * step)) % 2 == 1
        turned = list(parts)
        for p in range(4):
            if p & step:
                continue
            low, high = parts[p], parts[p + step]
            turned[p] = jnp.where(upper, pltpu.roll(high, step * block, 1), low)
            turned[p + step] = jnp.where(upper, high, pltpu.roll(low, LANES - step * block, 1))
        parts = turned
    return parts


def spread(x, wide_ref):
    wide_ref[...] = x.astype(jnp.float32).reshape(wide_ref.shape)


def arrange(wide_ref, turned_ref, channel, feeds):
    each = wide_ref.shape[0] // feeds
    high = each // 8
    block = turned_ref.shape[1] // feeds
    inner = LANES // block
    half = turned_ref.shape[0] // 2
    for first in range(0, feeds, inner):
        for r in range(2):
            parts = []
            for f in range(first, first + inner):
                start = f * each + 4 * channel + 2 * r
                both = [wide_ref[pl.ds(start + j, high, stride=8), :] for j in range(2)]
                parts.append(jnp.concatenate(both, axis=0).astype(jnp.bfloat16))
            for k, side in enumerate(lane_turn(parts, block)):
                row = r * half + 2 * k * high
                turned_ref[row : row + 2 * high, first * block : (first + inner) * block] = side


def product(a, b):
    return lax.dot_general(a, b, (((1,), (1,)), ((), ())), preferred_element_type=jnp.float32)


def order(turned_ref, place_ref, z_ref):
    inputs = place_ref.shape[0]
    frames = turned_ref.shape[0] // 2
    z = product(place_ref[...], turned_ref[...])
    z_ref[:inputs] = z.astype(jnp.bfloat16)
    z_ref[inputs:, :frames] = z[:, frames:].astype(jnp.bfloat16)
    z_ref[inputs:, frames:] = (-z[:, :frames]).astype(jnp.bfloat16)


def correlate(z_ref, out_ref, norm, r):
    inputs = z_ref.shape[1]
    part = slice(r * inputs, (r + 1) * inputs)
    out_ref[r] = norm * product(z_ref[part], z_ref[:inputs])


def gram_kernel(
    feeds, norm, upper_ref, x_ref, place_ref, out_ref, held_ref, wide_ref,
    turned0_ref, turned1_ref, z0_ref, z1_ref, done_ref, in_sems, out_sems,
):
    turned, z = (turned0_ref, turned1_ref), (z0_ref, z1_ref)
    pairs = x_ref.shape[1]
    channels = PAIR * pairs

    def fetch(pair):
        return pltpu.make_async_copy(x_ref.at[:, pair], held_ref.at[pair], in_sems.at[pair])

    def send(slot, r):
        low = SLOTS[slot]
        high = low if slot < PAIR else channels - low
        local = jnp.where(upper_ref[0] == 0, low, high)
        return pltpu.make_async_copy(
            done_ref.at[slot, r], out_ref.at[local, r], out_sems.at[slot, r]
        )

    fetch(0).start()
    for step in range(channels + 2):
        now = step % 2
        if step < channels and step % PAIR == 0:
            fetch(step // PAIR).wait()
            if step == 0:
                for pair in range(1, pairs):
                    fetch(pair).start()
        if step > 1:
            for r in range(2):
                correlate(z[now], done_ref.at[step - 2], norm, r)
                send(step - 2, r).start()
        if 0 < step <= channels:
            order(turned[1 - now], place_ref, z[1 - now])
        if step < channels:
            if step % PAIR == 0:
                spread(held_ref[step // PAIR], wide_ref)
            arrange(wide_ref, turned[now], step % PAIR, feeds)
    for slot in range(channels):
        for r in range(2):
            send(slot, r).wait()


def grams(upper, incoming, place, feeds):
    devices, pairs, groups, sub, _ = incoming.shape
    channels = PAIR * pairs
    inputs = place.shape[0]
    frames = devices * groups * sub * LANES // (2 * PAIR * inputs)
    return pl.pallas_call(
        functools.partial(gram_kernel, feeds, 1.0 / math.sqrt(frames)),
        in_specs=[
            pl.BlockSpec(memory_space=pltpu.SMEM),
            pl.BlockSpec(memory_space=pl.ANY),
            pl.BlockSpec(memory_space=pltpu.VMEM),
        ],
        out_specs=pl.BlockSpec(memory_space=pl.ANY),
        out_shape=jax.ShapeDtypeStruct((channels, 2, inputs, inputs), jnp.float32),
        scratch_shapes=[
            pltpu.VMEM((pairs, devices, groups, sub, LANES), jnp.bfloat16),
            pltpu.VMEM((devices * groups * sub, LANES), jnp.float32),
            pltpu.VMEM((2 * frames, inputs), jnp.bfloat16),
            pltpu.VMEM((2 * frames, inputs), jnp.bfloat16),
            pltpu.VMEM((2 * inputs, 2 * frames), jnp.bfloat16),
            pltpu.VMEM((2 * inputs, 2 * frames), jnp.bfloat16),
            pltpu.VMEM((channels, 2, inputs, inputs), jnp.float32),
            pltpu.SemaphoreType.DMA((pairs,)),
            pltpu.SemaphoreType.DMA((channels, 2)),
        ],
        compiler_params=pltpu.CompilerParams(vmem_limit_bytes=40 * MIB),
        cost_estimate=pl.CostEstimate(
            flops=channels * 12 * inputs * inputs * frames,
            bytes_accessed=channels * (8 * inputs * inputs + 4 * inputs * frames),
            transcendentals=0,
        ),
        name="gram",
    )(upper, *in_hbm(incoming), *in_vmem(place))


def per_device(samples, input_map):
    feeds = lax.axis_size("feed")
    times = lax.axis_size("tm")
    devices = feeds * times
    inputs = input_map.shape[0]
    taper = jnp.asarray(taper_table())
    table = jnp.asarray(transform_table(devices))
    last = samples[:, samples.shape[1] - HALO * NFFT :].astype(jnp.bfloat16)
    halo = lax.ppermute(last, "tm", [(t, t + 1) for t in range(times - 1)])
    place = (input_map[:, None] == jnp.arange(inputs)[None, :]).astype(jnp.bfloat16)
    device = lax.axis_index("feed") * times + lax.axis_index("tm")
    upper = (2 * device // devices).astype(jnp.int32).reshape(1)
    spectra, *held = head(samples, taper, table, devices)
    first, begin, curve, fixed = held
    outgoing = tail(begin, halo, first, curve, fixed, spectra)
    incoming = lax.all_to_all(outgoing, ("feed", "tm"), split_axis=0, concat_axis=0, tiled=True)
    return grams(upper, incoming, place, feeds)


def solution(mesh):
    in_specs = (P("feed", "tm"), P())
    out_specs = P(("feed", "tm"), None, None, None)
    return jax.shard_map(
        per_device, mesh=mesh, in_specs=in_specs, out_specs=out_specs, check_vma=False
    )
```

```python
import functools
import math

import jax
import jax.numpy as jnp
import ml_dtypes
import numpy as np
from jax import lax
from jax.experimental import pallas as pl
from jax.experimental.pallas import tpu as pltpu
from jax.sharding import PartitionSpec as P

CHANNELS = 1024
NFFT = 2048
HALF = NFFT // 2
TAPS = 4
HALO = TAPS - 1
LANES = 128
GROUP = 8
PAIR = 2
SLOTS = (0, 4, 1, 7, 2, 6, 3, 5)
EXTRA = 16
PARTS = (528, 512)
MIB = 1024 * 1024


def sample_order():
    chunk = 2 * LANES * np.arange(HALF // LANES)[:, None]
    lane = np.arange(LANES)[None, :]
    even = chunk + 2 * lane
    odd = chunk + (LANES + 2 * lane) % (2 * LANES) + 1
    return np.concatenate([even.reshape(-1), odd.reshape(-1)])


def taper_table():
    total = TAPS * NFFT
    place = np.arange(total).astype(np.float32)
    offset = (place - np.float32((total - 1) / 2.0)) / np.float32(NFFT)
    arg = np.float32(math.pi) * offset
    sinc = np.sin(arg) / arg
    window = np.float32(0.54) - np.float32(0.46) * np.cos(
        np.float32(2.0 * math.pi) * place / np.float32(total - 1)
    )
    return (sinc * window).astype(np.float32).reshape(TAPS, NFFT)[:, sample_order()]


def transform_table(devices):
    per = CHANNELS // devices
    slots = np.array([per if slot == 0 else slot for slot in SLOTS])
    channel = (per * np.arange(devices // 2)[:, None] + slots[None, :]).reshape(-1)
    channel = np.concatenate([np.zeros(EXTRA // 2, np.int64), channel])
    phase = (channel[:, None] * sample_order()[None, :] % NFFT).astype(np.float32)
    phase = phase * np.float32(2.0 * math.pi / NFFT)
    factor = np.float32((8.0 * NFFT) ** (-0.5))
    pair = np.stack([np.cos(phase) * factor, -np.sin(phase) * factor], axis=1)
    return pair.reshape(-1, NFFT).astype(ml_dtypes.bfloat16)


def separate(left, right):
    lane = lax.broadcasted_iota(jnp.int32, left.shape, 1)
    low = lane < LANES // 2
    even_first = jnp.where(low, 2 * lane, 2 * lane - LANES + 1)
    odd_first = jnp.where(low, 2 * lane + 1, 2 * lane - LANES)
    left = jnp.take_along_axis(left, even_first, axis=1, mode="promise_in_bounds")
    right = jnp.take_along_axis(right, odd_first, axis=1, mode="promise_in_bounds")
    return jnp.where(low, left, right), jnp.where(low, right, left)


def frame_part(ref, part, frame, chunk):
    both = []
    for side in range(2):
        start = frame * NFFT + (2 * chunk + side) * LANES
        both.append(ref[part, start : start + LANES].astype(jnp.float32))
    return separate(*both)


def filter_chunk(ref, frames, taper_ref, out_ref, place, chunk, past, keep=None):
    rows = ref.shape[0]
    lanes = [slice(side * HALF + chunk * LANES, side * HALF + (chunk + 1) * LANES) for side in range(2)]
    taper = [[taper_ref[tap : tap + 1, lane] for tap in range(TAPS)] for lane in lanes]
    for row in range(0, rows, 16):
        part = slice(row, row + 16)
        x = [past(t, part, chunk) for t in range(HALO)]
        for k in range(frames):
            x.append(frame_part(ref, part, k, chunk))
            for side in range(2):
                value = taper[side][0] * x[k][side]
                for tap in range(1, TAPS):
                    value = value + taper[side][tap] * x[k + tap][side]
                start = (place + k) * rows + row
                out_ref[start : start + 16, lanes[side]] = value.astype(jnp.bfloat16)
        if keep is not None:
            for t in range(HALO):
                keep(t, part, chunk, x[frames + t])


def transform_part(table_ref, filtered_ref, plus_ref, minus_ref, first, count):
    even, odd = (
        product(table_ref[first : first + count, lanes], filtered_ref[:, lanes])
        for lanes in (slice(0, HALF), slice(HALF, NFFT))
    )
    row = lax.broadcasted_iota(jnp.int32, (count, LANES), 0)
    sign = jnp.where(row % 2 == 0, 1.0, -1.0)
    total = even.shape[1] // LANES
    for j in range(total):
        e, o = (value[:, j * LANES : (j + 1) * LANES] for value in (even, odd))
        plus_ref[pl.ds(first * total + j, count, stride=total), :] = e + o
        minus_ref[pl.ds(first * total + j, count, stride=total), :] = sign * (e - o)


def pack_lower(plus_ref, out_ref):
    devices, pairs, sub, _ = out_ref.shape
    rows = pairs * sub
    half = devices // 2
    upper = plus_ref[rows:, :].reshape(half, pairs, sub, LANES)
    for p in range(1, pairs):
        out_ref[:half, p] = upper[:, p].astype(jnp.bfloat16)
    before = plus_ref[: half * rows, :].reshape(half, pairs, sub, LANES)[:, 0]
    place = lax.broadcasted_iota(jnp.int32, before.shape, 1)
    out_ref[:half, 0] = jnp.where(place < sub // PAIR, before, upper[:, 0]).astype(jnp.bfloat16)


def pack_upper(minus_ref, out_ref):
    devices, pairs, sub, _ = out_ref.shape
    rows = pairs * sub
    for d in range(devices // 2):
        tile = minus_ref[(d + 1) * rows : (d + 2) * rows, :]
        out_ref[devices - 1 - d] = tile.astype(jnp.bfloat16).reshape(pairs, sub, LANES)


def head_kernel(
    samples_ref, curve_ref, table_ref, out_ref, first_ref, begin_ref, taper_ref, fixed_ref,
    rest_ref, held_ref, carry_ref, filtered0_ref, filtered1_ref, plus0_ref, plus1_ref,
    minus0_ref, minus1_ref, packed0_ref, packed1_ref, in_sems, out_sems,
):
    groups = held_ref.shape[0] + 1
    filtered, packed = (filtered0_ref, filtered1_ref), (packed0_ref, packed1_ref)
    plus, minus = (plus0_ref, plus1_ref), (minus0_ref, minus1_ref)
    width = GROUP * NFFT

    def fetch(g):
        source = samples_ref.at[:, pl.ds(g * width, width)]
        return pltpu.make_async_copy(source, held_ref.at[g - 1], in_sems.at[g])

    def send(g):
        return pltpu.make_async_copy(packed[g % 2], out_ref.at[:, :, g], out_sems.at[g % 2])

    begin = pltpu.make_async_copy(
        samples_ref.at[:, pl.ds(0, HALO * NFFT)], begin_ref, in_sems.at[0]
    )
    rest = pltpu.make_async_copy(
        samples_ref.at[:, pl.ds(HALO * NFFT, (GROUP - HALO) * NFFT)], rest_ref, in_sems.at[groups]
    )
    table = pltpu.make_async_copy(table_ref, fixed_ref, in_sems.at[groups + 1])
    taper = pltpu.make_async_copy(curve_ref, taper_ref, in_sems.at[groups + 2])
    taper.start()
    rest.start()
    fetch(1).start()
    table.start()
    for g in range(2, groups):
        fetch(g).start()
    begin.start()

    def past(t, part, chunk):
        lane = 2 * t * HALF + chunk * LANES
        return tuple(carry_ref[part, lane + s * HALF : lane + s * HALF + LANES] for s in range(2))

    def keep(t, part, chunk, value):
        lane = 2 * t * HALF + chunk * LANES
        for s in range(2):
            carry_ref[part, lane + s * HALF : lane + s * HALF + LANES] = value[s]

    def past_in(t, part, chunk):
        return frame_part(rest_ref, part, GROUP - 2 * HALO + t, chunk)

    def past_own(t, part, chunk):
        return frame_part(begin_ref, part, t, chunk)

    chunks = HALF // LANES
    taper.wait()
    rest.wait()
    fetch(1).wait()
    for chunk in range(chunks):
        filter_chunk(held_ref.at[0], GROUP, taper_ref, filtered[1], 0, chunk, past_in, keep)
    table.wait()
    for g in range(1, groups):
        now = g % 2
        if g + 1 < groups:
            fetch(g + 1).wait()
        else:
            begin.wait()
        if g > 3:
            send(g - 3).wait()
        first = 0
        for i, count in enumerate(PARTS):
            transform_part(fixed_ref, filtered[now], plus[now], minus[now], first, count)
            first += count
            if g > 1:
                if i == 0:
                    pack_lower(plus[1 - now], packed[1 - now])
                if i == len(PARTS) - 1:
                    pack_upper(minus[1 - now], packed[1 - now])
            share = chunks // len(PARTS)
            for chunk in range(i * share, (i + 1) * share):
                if g + 1 < groups:
                    filter_chunk(
                        held_ref.at[g], GROUP, taper_ref, filtered[1 - now], 0, chunk, past, keep
                    )
                else:
                    filter_chunk(
                        rest_ref, GROUP - HALO, taper_ref, first_ref, HALO, chunk, past_own
                    )
        if g > 1:
            send(g - 1).start()
    last = (groups - 1) % 2
    send(groups - 3).wait()
    pack_lower(plus[last], packed[last])
    pack_upper(minus[last], packed[last])
    send(groups - 1).start()
    send(groups - 2).wait()
    send(groups - 1).wait()


def in_hbm(*values):
    return tuple(pltpu.with_memory_space_constraint(value, pltpu.HBM) for value in values)


def in_vmem(*values):
    return tuple(pltpu.with_memory_space_constraint(value, pltpu.VMEM) for value in values)


def head(samples, taper, table, devices):
    rows, length = samples.shape
    groups = length // (GROUP * NFFT)
    pairs = CHANNELS // devices // PAIR
    width = GROUP * rows
    sub = 2 * PAIR * width // LANES
    spectra = (devices, pairs, groups, sub, LANES)
    packed = pltpu.VMEM((devices, pairs, sub, LANES), jnp.bfloat16)
    filtered = pltpu.VMEM((width, NFFT), jnp.bfloat16)
    turned = pltpu.VMEM((table.shape[0] * width // LANES, LANES), jnp.float32)
    return pl.pallas_call(
        head_kernel,
        in_specs=[
            pl.BlockSpec(memory_space=pltpu.HBM),
            pl.BlockSpec(memory_space=pltpu.HBM),
            pl.BlockSpec(memory_space=pltpu.HBM),
        ],
        out_specs=[pl.BlockSpec(memory_space=pltpu.HBM)]
        + [pl.BlockSpec(memory_space=pltpu.VMEM)] * 4,
        out_shape=[
            pltpu.HBM(spectra, jnp.bfloat16),
            pltpu.VMEM((width, NFFT), jnp.bfloat16),
            pltpu.VMEM((rows, HALO * NFFT), jnp.int32),
            pltpu.VMEM(taper.shape, jnp.float32),
            pltpu.VMEM(table.shape, jnp.bfloat16),
        ],
        scratch_shapes=[
            pltpu.VMEM((rows, (GROUP - HALO) * NFFT), jnp.int32),
            pltpu.VMEM((groups - 1, rows, GROUP * NFFT), jnp.int32),
            pltpu.VMEM((rows, HALO * NFFT), jnp.float32),
            filtered, filtered, turned, turned, turned, turned, packed, packed,
            pltpu.SemaphoreType.DMA((groups + 3,)),
            pltpu.SemaphoreType.DMA((2,)),
        ],
        compiler_params=pltpu.CompilerParams(vmem_limit_bytes=40 * MIB),
        cost_estimate=pl.CostEstimate(
            flops=2 * table.shape[0] * NFFT * width * 3,
            bytes_accessed=2 * table.shape[0] * NFFT + 4 * rows * length,
            transcendentals=0,
        ),
        name="head",
    )(*in_hbm(samples, taper, table))


def tail_kernel(
    begin_ref, halo_ref, first_ref, taper_ref, fixed_ref, _, out_ref,
    filtered_ref, plus_ref, minus_ref, packed_ref, out_sems,
):
    rows = begin_ref.shape[0]
    kept = HALO * rows
    half = packed_ref.shape[0] // 2

    def past(t, part, chunk):
        return frame_part(halo_ref, part, t, chunk)

    def send(side):
        part = pl.ds(side * half, half)
        return pltpu.make_async_copy(packed_ref.at[part], out_ref.at[part, :, 0], out_sems.at[side])

    filtered_ref[kept:, :] = first_ref[kept:, :]
    for chunk in range(HALF // LANES):
        filter_chunk(begin_ref, HALO, taper_ref, filtered_ref, 0, chunk, past)
    first = 0
    for count in PARTS:
        transform_part(fixed_ref, filtered_ref, plus_ref, minus_ref, first, count)
        first += count
    pack_lower(plus_ref, packed_ref)
    send(0).start()
    pack_upper(minus_ref, packed_ref)
    send(1).start()
    send(0).wait()
    send(1).wait()


def tail(begin, halo, first, taper, fixed, spectra):
    rows = begin.shape[0]
    width = GROUP * rows
    devices, pairs, _, sub, _ = spectra.shape
    turned = pltpu.VMEM((fixed.shape[0] * width // LANES, LANES), jnp.float32)
    return pl.pallas_call(
        tail_kernel,
        in_specs=[pl.BlockSpec(memory_space=pltpu.VMEM)] * 5
        + [pl.BlockSpec(memory_space=pltpu.HBM)],
        out_specs=pl.BlockSpec(memory_space=pltpu.HBM),
        out_shape=pltpu.HBM(spectra.shape, spectra.dtype),
        scratch_shapes=[
            pltpu.VMEM((width, NFFT), jnp.bfloat16),
            turned, turned,
            pltpu.VMEM((devices, pairs, sub, LANES), jnp.bfloat16),
            pltpu.SemaphoreType.DMA((2,)),
        ],
        input_output_aliases={5: 0},
        compiler_params=pltpu.CompilerParams(vmem_limit_bytes=32 * MIB),
        cost_estimate=pl.CostEstimate(
            flops=2 * fixed.shape[0] * NFFT * width,
            bytes_accessed=2 * fixed.shape[0] * NFFT,
            transcendentals=0,
        ),
        name="tail",
    )(*in_vmem(begin, halo, first, taper, fixed), *in_hbm(spectra))


def lane_turn(parts, block):
    lane = lax.broadcasted_iota(jnp.int32, parts[0].shape, 1)
    for step in (2, 1):
        upper = (lane // (block * step)) % 2 == 1
        turned = list(parts)
        for p in range(4):
            if p & step:
                continue
            low, high = parts[p], parts[p + step]
            turned[p] = jnp.where(upper, pltpu.roll(high, step * block, 1), low)
            turned[p + step] = jnp.where(upper, high, pltpu.roll(low, LANES - step * block, 1))
        parts = turned
    return parts


def spread(x, wide_ref):
    wide_ref[...] = x.astype(jnp.float32).reshape(wide_ref.shape)


def arrange(wide_ref, turned_ref, channel, feeds):
    each = wide_ref.shape[0] // feeds
    high = each // 8
    block = turned_ref.shape[1] // feeds
    inner = LANES // block
    half = turned_ref.shape[0] // 2
    for first in range(0, feeds, inner):
        for r in range(2):
            parts = []
            for f in range(first, first + inner):
                start = f * each + 4 * channel + 2 * r
                both = [wide_ref[pl.ds(start + j, high, stride=8), :] for j in range(2)]
                parts.append(jnp.concatenate(both, axis=0).astype(jnp.bfloat16))
            for k, side in enumerate(lane_turn(parts, block)):
                row = r * half + 2 * k * high
                turned_ref[row : row + 2 * high, first * block : (first + inner) * block] = side


def product(a, b):
    return lax.dot_general(a, b, (((1,), (1,)), ((), ())), preferred_element_type=jnp.float32)


def order(turned_ref, place_ref, z_ref):
    inputs = place_ref.shape[0]
    frames = turned_ref.shape[0] // 2
    z = product(place_ref[...], turned_ref[...])
    z_ref[:inputs] = z.astype(jnp.bfloat16)
    z_ref[inputs:, :frames] = z[:, frames:].astype(jnp.bfloat16)
    z_ref[inputs:, frames:] = (-z[:, :frames]).astype(jnp.bfloat16)


def correlate(z_ref, out_ref, norm):
    inputs = z_ref.shape[1]
    half = inputs // 2
    left = norm * product(z_ref[...], z_ref[:half])
    below = jnp.concatenate([z_ref[half:inputs], z_ref[inputs + half :]], axis=0)
    right = norm * product(below, z_ref[half:inputs])
    for r in range(2):
        corner = left[r * inputs + half : (r + 1) * inputs]
        out_ref[r, :half, :half] = left[r * inputs : r * inputs + half]
        out_ref[r, half:, :half] = corner
        out_ref[r, half:, half:] = right[r * half : (r + 1) * half]
        out_ref[r, :half, half:] = corner.T if r == 0 else -corner.T


def gram_kernel(
    feeds, norm, upper_ref, x_ref, place_ref, out_ref, held_ref, wide_ref,
    turned0_ref, turned1_ref, z0_ref, z1_ref, done_ref, in_sems, out_sems,
):
    turned, z = (turned0_ref, turned1_ref), (z0_ref, z1_ref)
    pairs = x_ref.shape[1]
    channels = PAIR * pairs

    def fetch(pair):
        return pltpu.make_async_copy(x_ref.at[:, pair], held_ref.at[pair], in_sems.at[pair])

    def send(slot, r):
        low = SLOTS[slot]
        high = low if slot < PAIR else channels - low
        local = jnp.where(upper_ref[0] == 0, low, high)
        return pltpu.make_async_copy(
            done_ref.at[slot, r], out_ref.at[local, r], out_sems.at[slot, r]
        )

    fetch(0).start()
    for step in range(channels + 2):
        now = step % 2
        if step < channels and step % PAIR == 0:
            fetch(step // PAIR).wait()
            if step == 0:
                for pair in range(1, pairs):
                    fetch(pair).start()
        if step > 1:
            correlate(z[now], done_ref.at[step - 2], norm)
            for r in range(2):
                send(step - 2, r).start()
        if 0 < step <= channels:
            order(turned[1 - now], place_ref, z[1 - now])
        if step < channels:
            if step % PAIR == 0:
                spread(held_ref[step // PAIR], wide_ref)
            arrange(wide_ref, turned[now], step % PAIR, feeds)
    for slot in range(channels):
        for r in range(2):
            send(slot, r).wait()


def grams(upper, incoming, place, feeds):
    devices, pairs, groups, sub, _ = incoming.shape
    channels = PAIR * pairs
    inputs = place.shape[0]
    frames = devices * groups * sub * LANES // (2 * PAIR * inputs)
    return pl.pallas_call(
        functools.partial(gram_kernel, feeds, 1.0 / math.sqrt(frames)),
        in_specs=[
            pl.BlockSpec(memory_space=pltpu.SMEM),
            pl.BlockSpec(memory_space=pl.ANY),
            pl.BlockSpec(memory_space=pltpu.VMEM),
        ],
        out_specs=pl.BlockSpec(memory_space=pl.ANY),
        out_shape=jax.ShapeDtypeStruct((channels, 2, inputs, inputs), jnp.float32),
        scratch_shapes=[
            pltpu.VMEM((pairs, devices, groups, sub, LANES), jnp.bfloat16),
            pltpu.VMEM((devices * groups * sub, LANES), jnp.float32),
            pltpu.VMEM((2 * frames, inputs), jnp.bfloat16),
            pltpu.VMEM((2 * frames, inputs), jnp.bfloat16),
            pltpu.VMEM((2 * inputs, 2 * frames), jnp.bfloat16),
            pltpu.VMEM((2 * inputs, 2 * frames), jnp.bfloat16),
            pltpu.VMEM((channels, 2, inputs, inputs), jnp.float32),
            pltpu.SemaphoreType.DMA((pairs,)),
            pltpu.SemaphoreType.DMA((channels, 2)),
        ],
        compiler_params=pltpu.CompilerParams(vmem_limit_bytes=40 * MIB),
        cost_estimate=pl.CostEstimate(
            flops=channels * 12 * inputs * inputs * frames,
            bytes_accessed=channels * (8 * inputs * inputs + 4 * inputs * frames),
            transcendentals=0,
        ),
        name="gram",
    )(upper, *in_hbm(incoming), *in_vmem(place))


def per_device(samples, input_map):
    feeds = lax.axis_size("feed")
    times = lax.axis_size("tm")
    devices = feeds * times
    inputs = input_map.shape[0]
    taper = jnp.asarray(taper_table())
    table = jnp.asarray(transform_table(devices))
    last = samples[:, samples.shape[1] - HALO * NFFT :].astype(jnp.bfloat16)
    halo = lax.ppermute(last, "tm", [(t, t + 1) for t in range(times - 1)])
    place = (input_map[:, None] == jnp.arange(inputs)[None, :]).astype(jnp.bfloat16)
    device = lax.axis_index("feed") * times + lax.axis_index("tm")
    upper = (2 * device // devices).astype(jnp.int32).reshape(1)
    spectra, *held = head(samples, taper, table, devices)
    first, begin, curve, fixed = held
    outgoing = tail(begin, halo, first, curve, fixed, spectra)
    incoming = lax.all_to_all(outgoing, ("feed", "tm"), split_axis=0, concat_axis=0, tiled=True)
    return grams(upper, incoming, place, feeds)


def solution(mesh):
    in_specs = (P("feed", "tm"), P())
    out_specs = P(("feed", "tm"), None, None, None)
    return jax.shard_map(
        per_device, mesh=mesh, in_specs=in_specs, out_specs=out_specs, check_vma=False
    )
```
